32 devices in a mesh: ctx: 8 (over y, x, core), exp: 4 (over z).
Axes of the slice: x: 2, y: 2, z: 4, core: 2. Of those that a mesh axis runs over, the one named last changes fastest.
Arguments:
- block_input: bfloat16 [512, 2, 768], P('ctx'), may hold values from -6 to 6
- output_cotangent: bfloat16 [512, 2, 768], P(('ctx', 'exp')), may hold values from -6 to 6
- attn_gain: float32 [768], replicated, may hold values from 0.5 to 1.5
- query_weight: bfloat16 [768, 768], P('ctx', 'exp'), may hold values from -0.21875 to 0.21875
- key_weight: bfloat16 [768, 768], P('ctx', 'exp'), may hold values from -0.21875 to 0.21875
- value_weight: bfloat16 [768, 768], P('ctx', 'exp'), may hold values from -0.21875 to 0.21875
- output_weight: bfloat16 [768, 768], P('exp', 'ctx'), may hold values from -6 to 6
- bias_table: float32 [32, 12], replicated, may hold values from -6 to 6
- buckets: int32 [512], replicated, may hold values from 0 to 31
- ffn_gain: float32 [768], replicated, may hold values from 0.5 to 1.5
- router_weight: float32 [768, 4], replicated, may hold values from -0.15625 to 0.15625
- routes: int32 [512, 2, 2], P(('ctx', 'exp')), may hold values from 0 to 3, all different within a row; in each aligned block of 32 rows (0 to 31, 32 to 63, ..., all dimensions but the last counted through in order) at most 24 rows name the same one
- route_prior: float32 [512, 2, 2], P(('ctx', 'exp')), may hold values from 0.5 to 2
- gate_weight: bfloat16 [4, 768, 3072], P('exp', 'ctx'), may hold values from -0.21875 to 0.21875
- up_weight: bfloat16 [4, 768, 3072], P('exp', 'ctx'), may hold values from -0.21875 to 0.21875
- down_weight: bfloat16 [4, 3072, 768], P('exp', 'ctx'), may hold values from -0.109375 to 0.109375
Outputs:
- block_output: bfloat16 [512, 2, 768], P(('ctx', 'exp'))
- input_grad: float32 [512, 2, 768], P(('ctx', 'exp'))
- attn_gain_grad: float32 [768], replicated
- query_grad: float32 [768, 768], P('ctx', 'exp')
- key_grad: float32 [768, 768], P('ctx', 'exp')
- value_grad: float32 [768, 768], P('ctx', 'exp')
- output_grad: float32 [768, 768], P('exp', 'ctx')
- table_grad: float32 [32, 12], replicated
- ffn_gain_grad: float32 [768], replicated
- router_grad: float32 [768, 4], replicated
- gate_grad: float32 [4, 768, 3072], P('exp', 'ctx')
- up_grad: float32 [4, 768, 3072], P('exp', 'ctx')
- down_grad: float32 [4, 3072, 768], P('exp', 'ctx')
The draws below stay inside these ranges and needn't reach their ends.
Inputs may be any that keep to these rules, and one draw needn't show every extreme that they name: `routes`: each token names two different experts. Taking positions in order with both sequences of a position together, every aligned block of 32 rows names no expert more than 24 times, a bound that some block reaches.
All inputs are finite; a program needn't handle non-finite values.
Results may differ from the reference program's by a relative error of at most 0.03.
Values may be sent and summed in bfloat16 or wider, within the bound.
No kernel may reach another device: no remote copies, remote signals or barrier semaphores. Data moves between devices by JAX's collectives and lax.ppermute only.
A program may use at most 320 MiB of HBM per device.

```python
import math
from functools import partial
import jax
import jax.numpy as jnp
import numpy as np
from jax import lax

D = 768
H = 12
HD = 64
FF = 3072
BUCKETS = 32
SEQS = 2
LEN = 512
EXPERTS = 4
ROWS = 32
CAP = 24


def place_ends(array, key, low, largest):
    shape = array.shape
    place = [jax.random.randint(jax.random.fold_in(key, axis), (), 0, shape[axis]) for axis in range(len(shape))]
    array = array.at[tuple(place)].set(low)
    longest = shape.index(max(shape))
    place[longest] = (place[longest] + 1) % shape[longest]
    return array.at[tuple(place)].set(largest)


def steps_of(key, extent, cuts, low, high):
    factor_of = 1.0
    for position, parts in cuts:
        heights = jax.random.uniform(jax.random.fold_in(jax.random.fold_in(key, 6), position), (parts,), jnp.float32, low / len(cuts), high / len(cuts))
        factor_of = factor_of * jnp.repeat(jnp.exp(heights), extent[position] // parts).reshape((-1,) + (1,) * (len(extent) - 1 - position))
    return factor_of


def routed_block(key, own, number, rows, count, top, most, lean):
    ranking = jax.random.permutation(key, count)
    crowded, common = shares(count, rows * top, most, lean, True), shares(count, rows * top, most, lean, False)
    places = jnp.arange(count)

    def named(tallies, offset_by):
        used = int((tallies > 0).sum())
        fixed = max(1, used // 4)
        moved = fixed + (places - fixed + offset_by * (used - fixed)) % max(1, count - fixed)
        return jnp.zeros((count,), jnp.int32).at[ranking[jnp.where(places < fixed, places, moved)]].set(jnp.asarray(tallies, jnp.int32))

    tallies = jnp.where(number % 4 == 0, named(crowded, number // 4), named(common, number - number // 4 - 1))
    mixed = jax.random.permutation(jax.random.fold_in(own, 3), count)
    giver, sink = mixed[0:count // 2 * 2:2], mixed[1:count // 2 * 2:2]
    margin = jnp.minimum(tallies[giver] - 1, most - tallies[sink]) // 2
    margin = jnp.where((giver == ranking[0]) | (sink == ranking[0]) | (tallies[sink] == 0), 0, jnp.maximum(margin, 0))
    moved = jax.random.randint(jax.random.fold_in(own, 4), (count // 2,), 0, 1 << 20) % (margin + 1)
    tallies = tallies.at[giver].add(-moved).at[sink].add(moved)
    members = jnp.searchsorted(jnp.cumsum(tallies), jnp.arange(rows * top), side="right").astype(jnp.int32)
    grid = members.reshape(top, rows).T
    grid = grid[jax.random.permutation(jax.random.fold_in(own, 1), rows)]
    offset_by = jax.random.randint(jax.random.fold_in(own, 2), (rows, 1), 0, top)
    return jnp.take_along_axis(grid, (jnp.arange(top)[None, :] + offset_by) % top, axis=1)


def shares(amount, total, most, skew, full):
    weights = [(1 << 20) // math.isqrt(standing ** skew) + 1 for standing in range(1, amount + 1)]
    largest = most if full else min(most, max(-(-total // amount), total * weights[0] // sum(weights)))
    least = 1 if total - largest >= amount - 1 else 0
    given, surplus = [largest] + [least] * (amount - 1), total - largest - least * (amount - 1)
    while surplus > 0:
        movable = [i for i in range(1, amount) if given[i] < largest] or [i for i in range(1, amount) if given[i] < most]
        whole, budget = sum([weights[i] for i in movable]), surplus
        for i in movable:
            more = min(most - given[i], max(1, budget * weights[i] // whole), surplus)
            given[i] = given[i] + more
            surplus = surplus - more
    return np.array(given)


def centred(stream_key, shape, deviation, bound, split=(), kind=jnp.bfloat16):
    drawn = jax.random.normal(stream_key, shape, jnp.float32) * deviation
    if len(split) > 0:
        drawn = steps_of(stream_key, shape, split, -0.22, 0.18) * drawn
    return jnp.clip(drawn, min=-bound, max=bound).astype(kind)


def setup_inputs(seed: int = 0) -> dict:
    key_list = jax.random.split(jax.random.key(seed), 17)
    block_input = centred(key_list[0], (LEN, SEQS, D), 1.0, 6.0, ((0, 8),))
    output_cotangent = centred(key_list[1], (LEN, SEQS, D), 1.0, 6.0, ((0, 32),))
    attn_gain = jnp.clip(1.0 + 0.1 * jax.random.normal(key_list[2], (D,), jnp.float32), 0.5, 1.5)
    query_weight = centred(key_list[3], (D, H * HD), D ** -0.5, 0.21875, ((0, 8), (1, 4)))
    key_weight = centred(key_list[4], (D, H * HD), D ** -0.5, 0.21875, ((0, 8), (1, 4)))
    value_weight = centred(key_list[5], (D, H * HD), D ** -0.5, 0.21875, ((0, 8), (1, 4)))
    output_weight = centred(key_list[6], (H * HD, D), 1 ** -0.5, 6.0, ((0, 4), (1, 8)))
    bias_table = centred(key_list[7], (BUCKETS, H), 1.0, 6.0, (), jnp.float32)
    buckets = place_ends(jax.random.randint(key_list[8], (LEN,), 0, BUCKETS), jax.random.fold_in(key_list[8], 1), 0, BUCKETS - 1).astype(jnp.int32)
    ffn_gain = jnp.clip(1.0 + 0.1 * jax.random.normal(key_list[9], (D,), jnp.float32), 0.5, 1.5)
    router_weight = centred(key_list[10], (D, EXPERTS), (2 * D) ** -0.5, 0.15625, (), jnp.float32)
    routes_keys = jax.random.split(jax.random.fold_in(key_list[11], 1), LEN * SEQS // ROWS)
    routes_turns = jax.random.permutation(jax.random.fold_in(key_list[11], 3), LEN * SEQS // ROWS)
    routes = jax.vmap(lambda own, number: routed_block(jax.random.fold_in(key_list[11], 2), own, number, ROWS, EXPERTS, 2, CAP, 1))(routes_keys, routes_turns).reshape((LEN, SEQS, 2))
    route_prior = jnp.clip(jnp.exp(math.log(2.0) - 1.3862944 * jax.random.uniform(key_list[12], (LEN, SEQS, 2), jnp.float32) ** steps_of(key_list[12], (LEN, SEQS, 2), ((0, 32),), -0.2, 0.2)), 0.5, 2.0)
    gate_weight = centred(key_list[13], (EXPERTS, D, FF), D ** -0.5, 0.21875, ((0, 4), (1, 8)))
    up_weight = centred(key_list[14], (EXPERTS, D, FF), D ** -0.5, 0.21875, ((0, 4), (1, 8)))
    down_weight = centred(key_list[15], (EXPERTS, FF, D), FF ** -0.5, 0.109375, ((0, 4), (1, 8)))
    return dict(block_input=block_input, output_cotangent=output_cotangent, attn_gain=attn_gain, query_weight=query_weight, key_weight=key_weight, value_weight=value_weight, output_weight=output_weight, bias_table=bias_table, buckets=buckets, ffn_gain=ffn_gain, router_weight=router_weight, routes=routes, route_prior=route_prior, gate_weight=gate_weight, up_weight=up_weight, down_weight=down_weight)


EPS = 1e-06
HIGH = lax.Precision.HIGHEST
FLOOR = -1e+30

@jax.custom_vjp
def low(v):
    return lax.optimization_barrier(v.astype(jnp.bfloat16)).astype(jnp.float32)

@jax.custom_vjp
def low_back(v):
    return v

def low_keep(v):
    return (low(v), None)

def low_pass(kept, grad):
    return (grad,)

def back_keep(v):
    return (v, None)

def back_low(kept, grad):
    return (low(grad),)
low.defvjp(low_keep, low_pass)
low_back.defvjp(back_keep, back_low)

def attend(queries, keys, values, bias_tab, buckets):
    block = min(512, LEN)
    score_scale = HD ** (-0.5)
    key_pos = jnp.arange(LEN, dtype=jnp.int32)

    def query_block(offset):
        chosen = lax.dynamic_slice_in_dim(queries, offset, block, 0)
        scores = jnp.einsum('qhd,khd->hqk', chosen, keys, precision=HIGH) * score_scale
        distance = offset + jnp.arange(block, dtype=jnp.int32)[:, None] - key_pos[None, :]
        bucket_ids = buckets[jnp.clip(distance, 0, LEN - 1)]
        scores = scores + jnp.transpose(bias_tab[bucket_ids], (2, 0, 1))
        scores = low_back(scores)
        scores = jnp.where((distance >= 0)[None], scores, FLOOR)
        probs = jax.nn.softmax(scores, axis=-1)
        return jnp.einsum('hqk,khd->qhd', low(probs), values, precision=HIGH)
    offsets = jnp.arange(LEN // block, dtype=jnp.int32) * block
    attended = lax.map(jax.checkpoint(query_block), offsets)
    return attended.reshape(LEN, H * HD)

def expert_block(packed, gate_weight, up_weight, down_weight):
    normed, gate_mat = packed
    combined = jnp.zeros(normed.shape, jnp.float32)
    for expert in range(EXPERTS):
        inputs = low_back(normed)
        gate_pre = low_back(jnp.dot(inputs, gate_weight[expert], precision=HIGH))
        up_pre = low_back(jnp.dot(inputs, up_weight[expert], precision=HIGH))
        hidden = low(jax.nn.gelu(gate_pre) * up_pre)
        result = low(low_back(jnp.dot(hidden, down_weight[expert], precision=HIGH)))
        combined = combined + gate_mat[:, expert:expert + 1] * result
    return combined

def layer(block_input, attn_gain, query_weight, key_weight, value_weight, output_weight, bias_table, ffn_gain, router_weight, gate_weight, up_weight, down_weight, buckets, routes, route_prior):
    scale_one = lax.rsqrt(lax.optimization_barrier(jnp.mean(block_input * block_input, axis=-1, keepdims=True)) + EPS)
    normed_one = low(block_input * scale_one * attn_gain)
    queries = low(low_back(jnp.einsum('tsd,dh->tsh', normed_one, query_weight, precision=HIGH)))
    keys = low(low_back(jnp.einsum('tsd,dh->tsh', normed_one, key_weight, precision=HIGH)))
    values = low(low_back(jnp.einsum('tsd,dh->tsh', normed_one, value_weight, precision=HIGH)))
    per_seq = []
    for seq in range(SEQS):
        per_seq.append(attend(queries[:, seq].reshape(LEN, H, HD), keys[:, seq].reshape(LEN, H, HD), values[:, seq].reshape(LEN, H, HD), bias_table, buckets))
    attended = low(low_back(jnp.stack(per_seq, axis=1)))
    attn_out = low_back(jnp.einsum('tsh,hd->tsd', attended, output_weight, precision=HIGH))
    resid = block_input + attn_out
    scale_two = lax.rsqrt(lax.optimization_barrier(jnp.mean(resid * resid, axis=-1, keepdims=True)) + EPS)
    normed_two = low(resid * scale_two * ffn_gain)
    flat = normed_two.reshape(LEN * SEQS, D)
    logits = jnp.dot(flat, router_weight, precision=HIGH)
    onehot = (routes.reshape(-1, 2)[:, :, None] == jnp.arange(EXPERTS, dtype=jnp.int32)).astype(jnp.float32)
    chosen = lax.optimization_barrier(jnp.sum(onehot * logits[:, None, :], axis=-1))
    gates = route_prior.reshape(-1, 2) * jax.nn.softmax(chosen, axis=-1)
    gate_mat = lax.optimization_barrier(jnp.sum(gates[:, :, None] * onehot, axis=1))
    row_block = min(4096, LEN * SEQS)
    count = LEN * SEQS // row_block
    mixed = lax.map(jax.checkpoint(partial(expert_block, gate_weight=gate_weight, up_weight=up_weight, down_weight=down_weight)), (flat.reshape(count, row_block, D), gate_mat.reshape(count, row_block, EXPERTS)))
    return resid + mixed.reshape(LEN, SEQS, D)

def reference(block_input, output_cotangent, attn_gain, query_weight, key_weight, value_weight, output_weight, bias_table, buckets, ffn_gain, router_weight, routes, route_prior, gate_weight, up_weight, down_weight):
    floats = [block_input, attn_gain, query_weight, key_weight, value_weight, output_weight, bias_table, ffn_gain, router_weight, gate_weight, up_weight, down_weight]
    floats = [item.astype(jnp.float32) for item in floats]
    prior = route_prior.astype(jnp.float32)

    def apply(inputs, gain_one, query_w, key_w, value_w, output_w, table, gain_two, router_w, gate_w, up_w, down_w):
        return layer(inputs, gain_one, query_w, key_w, value_w, output_w, table, gain_two, router_w, gate_w, up_w, down_w, buckets, routes, prior)
    result, pullback = jax.vjp(apply, *floats)
    grads = pullback(output_cotangent.astype(jnp.float32))
    return (result.astype(jnp.bfloat16), grads[0], grads[1], grads[2], grads[3], grads[4], grads[5], grads[6], grads[7], grads[8], grads[9], grads[10], grads[11])
```

```python
import functools

import jax
import jax.numpy as jnp
from jax import lax
from jax.experimental import pallas as pl
from jax.experimental.pallas import tpu as pltpu
from jax.sharding import PartitionSpec as P

HD = 64
EPS = 1e-06
FLOOR = -1e30
HIGH = lax.Precision.HIGHEST
F32 = jnp.float32
BF16 = jnp.bfloat16
LANES = 128
GELU_C = 0.7978845608028654
GELU_A = 0.044715


def swap(value, axis, bits):
    devices = lax.axis_size(axis)
    return lax.ppermute(value, axis, [(i, i ^ bits) for i in range(devices)])


def gather_ctx(value):
    devices = lax.axis_size("ctx")
    near = jnp.concatenate(
        [value[None]] + [swap(value, "ctx", 2 * j)[None] for j in range(1, devices // 2)], axis=0
    )
    return near, swap(near, "ctx", 1)


def reduce_ctx(near, far):
    got = swap(far, "ctx", 1)
    both = (near.astype(F32) + got.astype(F32)).astype(near.dtype)
    return [both[0]] + [swap(both[j], "ctx", 2 * j) for j in range(1, near.shape[0])]


def spread_exp(value):
    return [value] + [swap(value, "exp", d) for d in range(1, lax.axis_size("exp"))]


def nn(left, right, precision=None):
    return lax.dot_general(
        left, right, (((1,), (0,)), ((), ())), precision=precision, preferred_element_type=F32
    )


def nt(left, right, precision=None):
    return lax.dot_general(
        left, right, (((1,), (1,)), ((), ())), precision=precision, preferred_element_type=F32
    )


def tn(left, right, precision=None):
    return lax.dot_general(
        left, right, (((0,), (0,)), ((), ())), precision=precision, preferred_element_type=F32
    )


def call(body, name, outs, ids, *args, scratch=()):
    single = not isinstance(outs, list)
    specs = [pl.BlockSpec(memory_space=pltpu.SMEM)]
    specs += [pl.BlockSpec(memory_space=pltpu.VMEM)] * len(args)
    shapes = [jax.ShapeDtypeStruct(*o) for o in ([outs] if single else outs)]
    out_specs = [pl.BlockSpec(memory_space=pltpu.VMEM)] * len(shapes)
    return pl.pallas_call(
        body,
        out_shape=shapes[0] if single else shapes,
        in_specs=specs,
        out_specs=out_specs[0] if single else out_specs,
        scratch_shapes=list(scratch),
        compiler_params=pltpu.CompilerParams(vmem_limit_bytes=58 * 1024 * 1024),
        name=name,
    )(ids, *args)


def rms_scale(values):
    return lax.rsqrt(jnp.mean(values * values, axis=-1, keepdims=True) + EPS)


def iota(shape, axis):
    return lax.broadcasted_iota(jnp.int32, shape, axis)


def block_before(rows, tok, quarter):
    early, late = iota((rows, rows), 0), iota((rows, rows), 1)
    same = (early % tok) // quarter == (late % tok) // quarter
    return jnp.where(same & (early < late), 1.0, 0.0).astype(BF16)


def slot_hot(route0, route1, expert, before, tok, quarter, cap, parts):
    rows = route0.shape[1]
    named = (route0 == expert) | (route1 == expert)
    flags = jnp.broadcast_to(jnp.where(named, 1.0, 0.0), (16, rows)).astype(BF16)
    rank = nn(flags, before)[0:1].astype(jnp.int32)
    block = (iota((1, rows), 1) % tok) // quarter
    place = jnp.where(named, block * cap + rank, -1)
    return iota((parts * cap, rows), 0) == place, named


def pack_body(quarter, ids, cot, info, out):
    width = out.shape[1]
    out[0:quarter, :] = cot[:, :width]
    out[quarter : 2 * quarter, :] = cot[:, width:]
    values = info[...]
    hi = values.astype(BF16)
    rest = values - hi.astype(F32)
    mid = rest.astype(BF16)
    low = (rest - mid.astype(F32)).astype(BF16)
    lanes = values.shape[1]
    eye = (iota((lanes, width), 0) == iota((lanes, width), 1)).astype(F32).astype(BF16)
    stacked = jnp.concatenate(
        [hi.astype(F32), mid.astype(F32), low.astype(F32), jnp.zeros((4, lanes), F32)], axis=0
    ).astype(BF16)
    out[2 * quarter :, :] = nn(stacked, eye).astype(BF16)


def early_body(tok, quarter, cap, ids, *refs):
    pieces, (cot_out, info_out, slots_out) = refs[:-3], refs[-3:]
    exp_pos = ids[1]
    rows = 2 * tok
    info = jnp.zeros((16, rows), F32)
    for d, piece in enumerate(pieces):
        owner = exp_pos ^ d
        for s in range(2):
            cot_out[pl.ds(pl.multiple_of(s * tok + owner * quarter, quarter), quarter), :] = piece[
                s * quarter : (s + 1) * quarter, :
            ]
        lane, row = iota((LANES, rows), 0), iota((LANES, rows), 1)
        target = (lane // quarter) * tok + owner * quarter + lane % quarter
        spot = jnp.where((target == row) & (lane < 2 * quarter), 1.0, 0.0).astype(BF16)
        info = info + nn(piece[2 * quarter :, :LANES], spot)
    low = info[0:4] + (info[4:8] + info[8:12])
    info_out[...] = jnp.concatenate([low, jnp.zeros((4, rows), F32)], axis=0)
    before = block_before(rows, tok, quarter)
    hot, _ = slot_hot(
        low[0:1].astype(jnp.int32),
        low[1:2].astype(jnp.int32),
        exp_pos,
        before,
        tok,
        quarter,
        cap,
        len(pieces),
    )
    slots_out[...] = nn(jnp.where(hot, 1.0, 0.0).astype(BF16), cot_out[...]).astype(BF16)


def project_body(aligned, head_local, ids, x, gain, near, far, q_out, kv_out, a_out, w_out, out_t):
    ctx_pos = ids[0]
    tok, width = x.shape[0], gain.shape[1]
    if aligned:
        count, rows, _ = near.shape
        for j in range(count):
            for par, ref in ((0, near), (1, far)):
                owner = ctx_pos ^ (2 * j + par)
                spot = pl.ds(pl.multiple_of(owner * rows, rows), rows)
                w_out[spot, :] = ref[j, :, : 3 * head_local]
                out_t[spot, :] = ref[j, :, 3 * head_local :]
    else:
        w_out[...] = near[:, : 3 * head_local]
        out_t[...] = near[:, 3 * head_local :]
    for s in range(2):
        piece = x[:, s * width : (s + 1) * width].astype(F32)
        a_out[s * tok : (s + 1) * tok, :] = (piece * rms_scale(piece) * gain[...]).astype(BF16)
    full = nn(a_out[...], w_out[...]).astype(BF16)
    q_out[...] = full[:, :head_local]
    kv_out[...] = full[:, head_local:]


def attend_body(
    heads, ids, q, near, far, table, rev, o_out, low_out, p_out, kv_out
):
    ctx_pos, exp_pos = ids[0], ids[1]
    count, rows, _ = near.shape
    tok = rows // 2
    hl = heads * HD
    seq_len = rev.shape[1]
    start = ctx_pos * tok
    for j in range(count):
        for par, ref in ((0, near), (1, far)):
            kv_out[ctx_pos ^ (2 * j + par)] = ref[j].reshape(2, tok, 2 * hl)
    buckets, head_total = table.shape
    pick = jnp.where(
        iota((8, head_total), 1) == exp_pos * heads + iota((8, head_total), 0), 1.0, 0.0
    )
    own_table = nt(pick, table[...], HIGH)
    hot = jnp.where(iota((buckets, seq_len), 0) == rev[...], 1.0, 0.0)
    bias = pltpu.roll(nn(own_table, hot, HIGH), start + 1, 1)
    open_keys = iota((tok, seq_len), 1) <= start + iota((tok, seq_len), 0)
    skewed = []
    for h in range(heads):
        wide = jnp.broadcast_to(bias[h : h + 1, :], (tok, seq_len))
        turned = pltpu.roll(wide, 0, 1, stride=1, stride_axis=0)
        skewed.append(jnp.where(open_keys, turned, FLOOR))
    for s in range(2):
        outs = []
        for h in range(heads):
            query = q[s * tok : (s + 1) * tok, h * HD : (h + 1) * HD]
            key = kv_out[:, s, :, h * HD : (h + 1) * HD].reshape(seq_len, HD)
            value = kv_out[:, s, :, hl + h * HD : hl + (h + 1) * HD].reshape(seq_len, HD)
            scores = nt(query, key) * (HD**-0.5) + skewed[h]
            top = jnp.max(scores, axis=-1, keepdims=True)
            weights = jnp.exp(scores - top)
            probs = weights * (1.0 / jnp.sum(weights, axis=-1, keepdims=True))
            p_out[s * heads + h] = probs
            outs.append(nn(probs.astype(BF16), value))
        out = jnp.concatenate(outs, axis=1)
        o_out[s * tok : (s + 1) * tok, :] = out
        low_out[s * tok : (s + 1) * tok, :] = out.astype(BF16)


def gate_values(logits, info):
    route0, route1 = info[0:1].astype(jnp.int32), info[1:2].astype(jnp.int32)
    choice0 = jnp.zeros_like(info[0:1])
    choice1 = jnp.zeros_like(info[0:1])
    for e in range(logits.shape[0]):
        choice0 = choice0 + jnp.where(route0 == e, logits[e : e + 1], 0.0)
        choice1 = choice1 + jnp.where(route1 == e, logits[e : e + 1], 0.0)
    top = jnp.maximum(choice0, choice1)
    up0, up1 = jnp.exp(choice0 - top), jnp.exp(choice1 - top)
    total = up0 + up1
    return up0 / total, up1 / total


def route_body(tok, quarter, cap, parts, ids, *refs):
    x = refs[0]
    lows, mats = refs[1 : 1 + parts], refs[1 + parts : 1 + 2 * parts]
    gain, router_t, info_ref, resid_out, gates_out, slots_out = refs[1 + 2 * parts :]
    exp_pos = ids[1]
    rows, width = 2 * tok, gain.shape[1]
    attn = nt(lows[0][...], mats[0][...])
    for d in range(1, parts):
        attn = attn + nt(lows[d][...], mats[d][...])
    for s in range(2):
        resid_out[s * tok : (s + 1) * tok, :] = (
            x[:, s * width : (s + 1) * width].astype(F32) + attn[s * tok : (s + 1) * tok]
        )
    resid = resid_out[...]
    normed = (resid * rms_scale(resid) * gain[...]).astype(BF16)
    logits = nt(router_t[...], normed.astype(F32), HIGH)
    info = info_ref[...]
    soft0, soft1 = gate_values(logits, info)
    gate0, gate1 = info[2:3] * soft0, info[3:4] * soft1
    gates_out[...] = jnp.concatenate([gate0, gate1, jnp.zeros((6, rows), F32)], axis=0)
    route0, route1 = info[0:1].astype(jnp.int32), info[1:2].astype(jnp.int32)
    before = block_before(rows, tok, quarter)
    hot, _ = slot_hot(route0, route1, exp_pos, before, tok, quarter, cap, parts)
    hot = jnp.where(hot, 1.0, 0.0).astype(BF16)
    first = route0 == exp_pos
    gate = jnp.where(first, gate0, gate1)
    slope = soft0 * soft1 * jnp.where(first, info[2:3], info[3:4])
    other = jnp.where(first, info[1:2], info[0:1])
    gate_hi, slope_hi = gate.astype(BF16).astype(F32), slope.astype(BF16).astype(F32)
    extras = jnp.concatenate(
        [gate_hi, gate - gate_hi, slope_hi, slope - slope_hi, other, jnp.zeros((LANES - 5, rows), F32)],
        axis=0,
    ).astype(BF16)
    slots_out[:, :width] = nn(hot, normed).astype(BF16)
    slots_out[:, width:] = nt(hot, extras).astype(BF16)


def expert_back_body(
    step, ids, x_near, x_far, c_near, c_far, w_in, down, router_t,
    dx_near, dx_far, hid_near, hid_far, dg_near, dg_far, du_near, du_far, router_out,
):
    exp_pos = ids[1]
    width, hidden = w_in.shape[0], down.shape[0]
    experts = router_t.shape[0]
    gate_w, up_w = w_in[:, :hidden], w_in[:, hidden:]
    down_w = down[...]
    own = jnp.zeros((1, width), F32)
    for e in range(experts):
        own = own + jnp.where(exp_pos == e, router_t[e : e + 1, :], 0.0)
    router_sum = jnp.zeros((8, width), F32)
    sides = (
        (x_near, c_near, dx_near, hid_near, dg_near, du_near),
        (x_far, c_far, dx_far, hid_far, dg_far, du_far),
    )
    for x, c, dx, hid, dg_out, du_out in sides:
        for lead in range(0, x.shape[0], step):
            part = slice(lead, lead + step)
            rows = x[part, :width]
            extras = x[part, width:].astype(F32)
            gate = extras[:, 0:1] + extras[:, 1:2]
            slope = extras[:, 2:3] + extras[:, 3:4]
            other = extras[:, 4:5].astype(jnp.int32)
            pre = nn(rows, gate_w)
            up = nn(rows, up_w)
            raw = nt(c[part, :], down_w)
            squared = pre * pre
            tanh = jnp.tanh(GELU_C * (pre + GELU_A * pre * squared))
            half = 0.5 * (1.0 + tanh)
            act = pre * half
            hidden_low = (act * up).astype(BF16)
            hid[part, :] = hidden_low
            slope_act = half + 0.5 * pre * (1.0 - tanh * tanh) * (
                GELU_C * (1.0 + 3.0 * GELU_A * squared)
            )
            gate_grad = jnp.sum(hidden_low.astype(F32) * raw, axis=-1, keepdims=True)
            grad = gate * raw
            dg = (grad * up * slope_act).astype(BF16)
            du = (grad * act).astype(BF16)
            dg_out[part, :] = dg
            du_out[part, :] = du
            tilt = gate_grad * slope
            kind = iota((step, 8), 1)
            spread = jnp.where(kind == exp_pos, tilt, 0.0) - jnp.where(kind == other, tilt, 0.0)
            back = nt(dg, gate_w) + nt(du, up_w) + tilt * own
            for e in range(experts):
                back = back - jnp.where(other == e, tilt, 0.0) * router_t[e : e + 1, :]
            dx[part, :] = back.astype(BF16)
            router_sum = router_sum + tn(spread, rows.astype(F32), HIGH)
    router_out[...] = router_sum


def expert_rest_body(
    step, ids, x_near, x_far, c_near, c_far, down, hid_near, hid_far, dg_near, dg_far, du_near, du_far,
    y_near, y_far, down_out, w_out,
):
    width, hidden = down.shape[1], down.shape[0]
    down_w = down[...]
    totals = [0.0, 0.0, 0.0]
    sides = (
        (x_near, c_near, hid_near, dg_near, du_near, y_near),
        (x_far, c_far, hid_far, dg_far, du_far, y_far),
    )
    for x, c, hid, dg, du, y in sides:
        for lead in range(0, x.shape[0], step):
            part = slice(lead, lead + step)
            rows = x[part, :width]
            extras = x[part, width:].astype(F32)
            gate = extras[:, 0:1] + extras[:, 1:2]
            y[part, :] = nn(hid[part, :], down_w).astype(BF16)
            dy = (gate * c[part, :].astype(F32)).astype(BF16)
            totals[0] = totals[0] + tn(hid[part, :], dy)
            totals[1] = totals[1] + tn(rows, dg[part, :])
            totals[2] = totals[2] + tn(rows, du[part, :])
    down_out[...] = totals[0]
    w_out[:, :hidden] = totals[1].astype(BF16)
    w_out[:, hidden:] = totals[2].astype(BF16)


def mix_body(tok, quarter, cap, parts, ids, resid, info_ref, gates_ref, y, out, held):
    exp_pos = ids[1]
    rows, width = 2 * tok, resid.shape[1]
    info, gates = info_ref[...], gates_ref[...]
    route0, route1 = info[0:1].astype(jnp.int32), info[1:2].astype(jnp.int32)
    before = block_before(rows, tok, quarter)
    block = (iota((1, rows), 1) % tok) // quarter
    weights = []
    for e in range(parts):
        named = ((route0 == e) | (route1 == e)) & (block == exp_pos)
        flags = jnp.broadcast_to(jnp.where(named, 1.0, 0.0), (16, rows)).astype(BF16)
        rank = jnp.where(named, nn(flags, before)[0:1].astype(jnp.int32), -1)
        gate = jnp.where(route0 == e, gates[0:1], gates[1:2])
        weights.append(jnp.where(iota((cap, rows), 0) == rank, gate, 0.0))
    weights = jnp.concatenate(weights, axis=0)
    hi = weights.astype(BF16)
    low = (weights - hi.astype(F32)).astype(BF16)
    held[...] = resid[...] + tn(hi, y[...]) + tn(low, y[...])
    for s in range(2):
        spot = pl.ds(pl.multiple_of(s * tok + exp_pos * quarter, quarter), quarter)
        out[:, s * width : (s + 1) * width] = held[spot, :].astype(BF16)


def attend_back_body(heads, tok, quarter, cap, parts, buckets, ids, *refs):
    pieces = refs[:parts]
    (
        resid_ref, cot, gain, info_ref, low, o, out_t, q, kv, p, rev,
        own_out, dq_out, near_out, far_out, dout_t, small_out, held, dkv,
    ) = refs[parts:]
    ctx_pos, exp_pos = ids[0], ids[1]
    rows, width = resid_ref.shape
    hl = heads * HD
    count = kv.shape[0]
    seq_len = count * tok
    start = ctx_pos * tok
    info = info_ref[...]
    route0, route1 = info[0:1].astype(jnp.int32), info[1:2].astype(jnp.int32)
    before = block_before(rows, tok, quarter)
    grad = jnp.zeros((rows, width), F32)
    for d, piece in enumerate(pieces):
        hot, _ = slot_hot(route0, route1, exp_pos ^ d, before, tok, quarter, cap, parts)
        grad = grad + tn(jnp.where(hot, 1.0, 0.0).astype(BF16), piece[...])
    resid = resid_ref[...]
    scale = rms_scale(resid)
    centred = resid * scale
    small_out[0:1, :] = jnp.sum(grad * centred, axis=0, keepdims=True) * (1.0 / parts)
    inner = grad * gain[...]
    held[...] = cot[...].astype(F32) + scale * (
        inner - centred * jnp.mean(inner * centred, axis=-1, keepdims=True)
    )
    for s in range(2):
        spot = pl.ds(pl.multiple_of(s * tok + exp_pos * quarter, quarter), quarter)
        own_out[s * quarter : (s + 1) * quarter, :] = held[spot, :]
    attn_grad = held[...].astype(BF16)
    grad_o = nn(attn_grad, out_t[...]).astype(BF16)
    dout_t[...] = tn(attn_grad, low[...]).astype(BF16)
    sums = [jnp.zeros((tok, seq_len), F32) for _ in range(heads)]
    for s in range(2):
        here = slice(s * tok, (s + 1) * tok)
        keys, values, queries = [], [], []
        for h in range(heads):
            cols = slice(h * HD, (h + 1) * HD)
            probs = p[s * heads + h]
            key = kv[:, s, :, cols].reshape(seq_len, HD)
            value = kv[:, s, :, hl + h * HD : hl + (h + 1) * HD].reshape(seq_len, HD)
            do = grad_o[here, cols]
            delta = jnp.sum(do.astype(F32) * o[here, cols], axis=-1, keepdims=True)
            ds = (probs * (nt(do, value) - delta)).astype(BF16)
            sums[h] = sums[h] + ds.astype(F32)
            values.append(tn(probs.astype(BF16), do))
            keys.append(tn(ds, q[here, cols]) * (HD**-0.5))
            queries.append(nn(ds, key) * (HD**-0.5))
        dq_out[here, :] = jnp.concatenate(queries, axis=1).astype(BF16)
        dkv[:, s] = (
            jnp.concatenate(keys + values, axis=1).astype(BF16).reshape(count, tok, 2 * hl)
        )
    for j in range(count // 2):
        near_out[j] = dkv[ctx_pos ^ (2 * j)].reshape(rows, 2 * hl)
        far_out[j] = dkv[ctx_pos ^ (2 * j + 1)].reshape(rows, 2 * hl)
    table = jnp.zeros((8, width), F32)
    for h in range(heads):
        turned = sums[h]
        step = 1
        while step < tok:
            bit = (iota((tok, seq_len), 0) // step) % 2 == 1
            turned = jnp.where(bit, pltpu.roll(turned, seq_len - step, 1), turned)
            step *= 2
        line = jnp.sum(turned, axis=0, keepdims=True)
        line = pltpu.roll(line, seq_len - start - 1, 1)
        spot = (exp_pos * heads + h) * buckets
        for lead in range(0, seq_len, 512):
            cut = slice(lead, min(lead + 512, seq_len))
            here = line[:, cut]
            hot = jnp.where(iota((here.shape[1], width), 1) == spot + rev[cut, :], 1.0, 0.0)
            table = table + nn(jnp.broadcast_to(here, (8, here.shape[1])), hot, HIGH)
    small_out[1:2, :] = table[0:1]
    small_out[2:8, :] = jnp.zeros((6, width), F32)


def back_project_body(quarter, parts, ids, *refs):
    terms = refs[:-10]
    dq, w, a, dout_t, x, gain, small, rows_out, w_near, small_out = refs[-10:]
    rows, width = a.shape
    tok = rows // 2
    dkv = terms[0][...].astype(F32)
    for term in terms[1:]:
        dkv = dkv + term[...].astype(F32)
    grads = jnp.concatenate([dq[...], dkv.astype(BF16)], axis=1)
    da = nt(grads, w[...])
    total = jnp.zeros((1, width), F32)
    for s in range(2):
        piece = x[:, s * width : (s + 1) * width].astype(F32)
        here = da[s * tok : (s + 1) * tok]
        total = total + jnp.sum(piece * rms_scale(piece) * here, axis=0, keepdims=True)
        for z in range(parts):
            rows_out[z, s * quarter : (s + 1) * quarter, :] = here[
                z * quarter : (z + 1) * quarter
            ].astype(BF16)
    wide = tn(a[...], grads)
    cut = grads.shape[1]
    w_near[:, :cut] = wide.astype(BF16)
    w_near[:, cut:] = dout_t[...]
    small_out[0:1, :] = total
    small_out[1:8, :] = small[1:8, :]


def finish_body(tok, quarter, ids, x, gain, own, mine, *refs):
    pieces, out = refs[:-1], refs[-1]
    exp_pos = ids[1]
    width = gain.shape[1]
    for s in range(2):
        spot = pl.ds(pl.multiple_of(exp_pos * quarter, quarter), quarter)
        rows = x[spot, s * width : (s + 1) * width].astype(F32)
        here = slice(s * quarter, (s + 1) * quarter)
        grad = mine[here, :].astype(F32)
        for piece in pieces:
            grad = grad + piece[here, :].astype(F32)
        scale = rms_scale(rows)
        centred = rows * scale
        inner = grad * gain[...]
        out[:, s * width : (s + 1) * width] = own[here, :] + scale * (
            inner - centred * jnp.mean(inner * centred, axis=-1, keepdims=True)
        )


def on_device(
    block_input,
    output_cotangent,
    attn_gain,
    query_weight,
    key_weight,
    value_weight,
    output_weight,
    bias_table,
    buckets,
    ffn_gain,
    router_weight,
    routes,
    route_prior,
    gate_weight,
    up_weight,
    down_weight,
):
    tok, seqs, width = block_input.shape
    quarter = routes.shape[0]
    ctx_size, parts = lax.axis_size("ctx"), lax.axis_size("exp")
    ctx_pos, exp_pos = lax.axis_index("ctx"), lax.axis_index("exp")
    hl = query_weight.shape[1]
    heads = hl // HD
    cap = (3 * quarter * seqs + 3) // 4
    slots = parts * cap
    rows = tok * seqs
    shard = query_weight.shape[0]
    hidden = down_weight.shape[1]
    half = ctx_size // 2
    seq_len = tok * ctx_size
    aligned = shard % 16 == 0
    ids = jnp.stack([ctx_pos, exp_pos]).astype(jnp.int32)
    x = block_input.reshape(tok, seqs * width)
    gain_one, gain_two = attn_gain.reshape(1, width), ffn_gain.reshape(1, width)
    router_t = router_weight.T
    rev = buckets[::-1].reshape(1, seq_len)

    packed = jnp.concatenate([query_weight, key_weight, value_weight, output_weight.T], axis=1)
    if aligned:
        w_near, w_far = gather_ctx(packed)
    else:
        w_near = lax.all_gather(packed, "ctx", axis=0, tiled=True)
        w_far = w_near[:8]

    sent = jnp.concatenate(
        [
            jnp.swapaxes(gate_weight.reshape(shard, ctx_size, hidden), 0, 1),
            jnp.swapaxes(up_weight.reshape(shard, ctx_size, hidden), 0, 1),
        ],
        axis=2,
    )
    w_in = lax.all_to_all(sent, "ctx", split_axis=0, concat_axis=0, tiled=True)
    w_in = w_in.reshape(width, 2 * hidden)
    down = down_weight.reshape(hidden, width)

    info = jnp.concatenate([routes.astype(F32), route_prior], axis=2)
    info = jnp.transpose(info, (2, 1, 0)).reshape(4, seqs * quarter)
    cot_pack = call(
        functools.partial(pack_body, quarter),
        "pack",
        ((2 * quarter + 16, width), BF16),
        ids,
        output_cotangent.reshape(quarter, seqs * width),
        info,
    )
    cot_block, info_block, cot_slots = call(
        functools.partial(early_body, tok, quarter, cap),
        "early_slots",
        [((rows, width), BF16), ((8, rows), F32), ((slots, width), BF16)],
        ids,
        *spread_exp(cot_pack),
    )

    q, kv, normed, w_qkv, out_t = call(
        functools.partial(project_body, aligned, hl),
        "project",
        [
            ((rows, hl), BF16),
            ((rows, 2 * hl), BF16),
            ((rows, width), BF16),
            ((width, 3 * hl), BF16),
            ((width, hl), BF16),
        ],
        ids, x, gain_one, w_near, w_far,
    )
    kv_near, kv_far = gather_ctx(kv)
    out_mats = spread_exp(out_t)
    c_near, c_far = gather_ctx(cot_slots)
    o, low, p, kv_all = call(
        functools.partial(attend_body, heads),
        "attend",
        [
            ((rows, hl), F32),
            ((rows, hl), BF16),
            ((seqs * heads, tok, seq_len), F32),
            ((ctx_size, seqs, tok, 2 * hl), BF16),
        ],
        ids, q, kv_near, kv_far, bias_table, rev,
    )
    lows = spread_exp(low)
    resid, gates, x_slots = call(
        functools.partial(route_body, tok, quarter, cap, parts),
        "route",
        [((rows, width), F32), ((8, rows), F32), ((slots, width + LANES), BF16)],
        ids, x, *lows, *out_mats, gain_two, router_t, info_block,
    )
    x_near, x_far = gather_ctx(x_slots)
    side = half * slots
    x_near, x_far = x_near.reshape(side, width + LANES), x_far.reshape(side, width + LANES)
    c_near, c_far = c_near.reshape(side, width), c_far.reshape(side, width)
    step = min(side, 4 * slots)
    (
        dx_near, dx_far, hid_near, hid_far, dg_near, dg_far, du_near, du_far, router_part,
    ) = call(
        functools.partial(expert_back_body, step),
        "expert_back",
        [((side, width), BF16)] * 2 + [((side, hidden), BF16)] * 6 + [((8, width), F32)],
        ids, x_near, x_far, c_near, c_far, w_in, down, router_t,
    )
    dx_terms = reduce_ctx(
        dx_near.reshape(half, slots, width), dx_far.reshape(half, slots, width)
    )
    y_near, y_far, down_grad, w_grad = call(
        functools.partial(expert_rest_body, step),
        "expert_rest",
        [
            ((side, width), BF16),
            ((side, width), BF16),
            ((hidden, width), F32),
            ((width, 2 * hidden), BF16),
        ],
        ids, x_near, x_far, c_near, c_far, down, hid_near, hid_far, dg_near, dg_far, du_near, du_far,
    )
    dx = sum(term.astype(F32) for term in dx_terms).astype(BF16)
    dx_pieces = spread_exp(dx)

    y_terms = reduce_ctx(y_near.reshape(half, slots, width), y_far.reshape(half, slots, width))
    y = sum(term.astype(F32) for term in y_terms).astype(BF16)
    y = lax.all_to_all(
        y.reshape(parts, cap, width), "exp", split_axis=0, concat_axis=0, tiled=True
    ).reshape(slots, width)
    block_output = call(
        functools.partial(mix_body, tok, quarter, cap, parts),
        "mix",
        ((quarter, seqs * width), BF16),
        ids, resid, info_block, gates, y,
        scratch=[pltpu.VMEM((rows, width), F32)],
    ).reshape(quarter, seqs, width)
    w_back = lax.all_to_all(
        w_grad.reshape(ctx_size, shard, 2 * hidden), "ctx", split_axis=0, concat_axis=0, tiled=True
    )
    w_back = jnp.swapaxes(w_back, 0, 1).astype(F32)
    gate_grad = w_back[:, :, :hidden].reshape(1, shard, ctx_size * hidden)
    up_grad = w_back[:, :, hidden:].reshape(1, shard, ctx_size * hidden)

    resid_grad, dq, dkv_near, dkv_far, dout_t, small = call(
        functools.partial(attend_back_body, heads, tok, quarter, cap, parts, bias_table.shape[0]),
        "attend_back",
        [
            ((seqs * quarter, width), F32),
            ((rows, hl), BF16),
            ((half, rows, 2 * hl), BF16),
            ((half, rows, 2 * hl), BF16),
            ((width, hl), BF16),
            ((8, width), F32),
        ],
        ids, *dx_pieces, resid, cot_block, gain_two, info_block, low, o, out_t, q, kv_all, p,
        rev.reshape(seq_len, 1),
        scratch=[
            pltpu.VMEM((rows, width), F32),
            pltpu.VMEM((ctx_size, seqs, tok, 2 * hl), BF16),
        ],
    )
    dkv_terms = reduce_ctx(dkv_near, dkv_far)
    small = jnp.concatenate([jnp.zeros((1, width), F32), small[0:2], router_part[:4], small[2:3]])
    da_parts, proj_grad, small = call(
        functools.partial(back_project_body, quarter, parts),
        "back_project",
        [
            ((parts, seqs * quarter, width), BF16),
            ((width, 4 * hl), BF16),
            ((8, width), F32),
        ],
        ids, *dkv_terms, dq, w_qkv, normed, dout_t, x, gain_one, small,
    )
    da_parts = [
        lax.dynamic_index_in_dim(da_parts, exp_pos ^ d, 0, keepdims=False) for d in range(parts)
    ]
    da_terms = [da_parts[0]] + [swap(da_parts[d], "exp", d) for d in range(1, parts)]
    input_grad = call(
        functools.partial(finish_body, tok, quarter),
        "finish",
        ((quarter, seqs * width), F32),
        ids, x, gain_one, resid_grad, *da_terms,
    ).reshape(quarter, seqs, width)

    proj_grad = proj_grad.reshape(ctx_size, shard, 4 * hl)
    near = jnp.stack([lax.dynamic_index_in_dim(proj_grad, ctx_pos ^ (2 * j), 0, False) for j in range(half)])
    far = jnp.stack(
        [lax.dynamic_index_in_dim(proj_grad, ctx_pos ^ (2 * j + 1), 0, False) for j in range(half)]
    )
    proj = sum(term.astype(F32) for term in reduce_ctx(near, far))

    small = sum(spread_exp(small))
    small = small + swap(small, "ctx", 1)
    small = small + sum(swap(small, "ctx", 2 * j) for j in range(1, half))
    head_total = bias_table.shape[1]
    table_grad = small[2, : head_total * bias_table.shape[0]].reshape(head_total, -1).T
    return (
        block_output,
        input_grad,
        small[0],
        proj[:, :hl],
        proj[:, hl : 2 * hl],
        proj[:, 2 * hl : 3 * hl],
        proj[:, 3 * hl :].T,
        table_grad,
        small[1],
        small[3:7].T,
        gate_grad,
        up_grad,
        down_grad.reshape(1, hidden, width),
    )


def solution(mesh):
    return jax.shard_map(
        on_device,
        mesh=mesh,
        in_specs=(
            P("ctx", None, None),
            P(("ctx", "exp"), None, None),
            P(),
            P("ctx", "exp"),
            P("ctx", "exp"),
            P("ctx", "exp"),
            P("exp", "ctx"),
            P(),
            P(),
            P(),
            P(),
            P(("ctx", "exp"), None, None),
            P(("ctx", "exp"), None, None),
            P("exp", "ctx", None),
            P("exp", "ctx", None),
            P("exp", "ctx", None),
        ),
        out_specs=(
            P(("ctx", "exp"), None, None),
            P(("ctx", "exp"), None, None),
            P(),
            P("ctx", "exp"),
            P("ctx", "exp"),
            P("ctx", "exp"),
            P("exp", "ctx"),
            P(),
            P(),
            P(),
            P("exp", "ctx", None),
            P("exp", "ctx", None),
            P("exp", "ctx", None),
        ),
        check_vma=False,
    )
```

```python
import functools

import jax
import jax.numpy as jnp
from jax import lax
from jax.experimental import pallas as pl
from jax.experimental.pallas import tpu as pltpu
from jax.sharding import PartitionSpec as P

HD = 64
EPS = 1e-06
FLOOR = -1e30
HIGH = lax.Precision.HIGHEST
F32 = jnp.float32
BF16 = jnp.bfloat16
LANES = 128
GELU_C = 0.7978845608028654
GELU_A = 0.044715


def swap(value, axis, bits):
    devices = lax.axis_size(axis)
    return lax.ppermute(value, axis, [(i, i ^ bits) for i in range(devices)])


def gather_ctx(value, after=()):
    devices = lax.axis_size("ctx")
    near = [value[None]] + [swap(value, "ctx", 2 * j)[None] for j in range(1, devices // 2)]
    if after:
        near = [hold(block, *after) for block in near]
    if devices > 8:
        near = [jnp.concatenate(near, axis=0)]
    return near + [swap(block, "ctx", 1) for block in near]


def each_block(refs):
    half = sum(ref.shape[0] for ref in refs) // 2
    listed = [(ref, i) for ref in refs for i in range(ref.shape[0])]
    return [(ref, i, 2 * (t % half) + t // half) for t, (ref, i) in enumerate(listed)]


def grouped(refs):
    listed = [(ref, i) for ref in refs for i in range(ref.shape[0])]
    return [listed[t : t + 4] for t in range(0, len(listed), 4)]


def stack(group, rows=slice(None), cols=slice(None)):
    return jnp.concatenate([ref[i, rows, cols] for ref, i in group], axis=0)


def trade_exp(value):
    return lax.all_to_all(value, "exp", split_axis=0, concat_axis=0, tiled=True)


def spread_exp(value):
    return [value] + [swap(value, "exp", d) for d in range(1, lax.axis_size("exp"))]


def nn(left, right, precision=None):
    return lax.dot_general(
        left, right, (((1,), (0,)), ((), ())), precision=precision, preferred_element_type=F32
    )


def nt(left, right, precision=None):
    return lax.dot_general(
        left, right, (((1,), (1,)), ((), ())), precision=precision, preferred_element_type=F32
    )


def tn(left, right, precision=None):
    return lax.dot_general(
        left, right, (((0,), (0,)), ((), ())), precision=precision, preferred_element_type=F32
    )


def room(shape, dtype):
    *lead, rows, cols = (1, 1, *shape)
    size = jnp.dtype(dtype).itemsize
    tile = 32 // size
    total = -(-rows // tile) * tile * -(-cols // LANES) * LANES * size
    for extent in lead:
        total *= extent
    return total


def call(body, name, outs, *args, us=2.0, scratch=(), after=(), wide=False, token=False):
    single = not isinstance(outs, list)
    outs = ([outs] if single else outs) + ([((8, LANES), F32)] if token else [])
    single = len(outs) == 1
    specs = [pl.BlockSpec(memory_space=pltpu.VMEM)] * len(args)
    specs += [
        pl.BlockSpec(memory_space=pltpu.VMEM if room(a.shape, a.dtype) <= 2**16 else pl.ANY)
        for a in after
    ]
    shapes = [jax.ShapeDtypeStruct(*o) for o in outs]
    out_specs = [pl.BlockSpec(memory_space=pltpu.VMEM)] * len(shapes)

    held = sum(room(a.shape, a.dtype) for a in (*args, *shapes))
    held += sum(room(a.shape, a.dtype) for a in scratch)
    limit = min(62 * 2**20, max(16 * 2**20 + 2 * held, 60 * 2**20 if wide else 0))

    def run(*refs):
        rest = refs[len(args) + len(after) :]
        if token:
            place = len(shapes) - 1
            rest[place][...] = jnp.zeros(rest[place].shape, F32)
            rest = rest[:place] + rest[place + 1 :]
        body(*refs[: len(args)], *rest)

    return pl.pallas_call(
        run,
        out_shape=shapes[0] if single else shapes,
        in_specs=specs,
        out_specs=out_specs[0] if single else out_specs,
        scratch_shapes=list(scratch),
        compiler_params=pltpu.CompilerParams(vmem_limit_bytes=limit),
        cost_estimate=pl.CostEstimate(flops=0, bytes_accessed=int(us * 3.0e4), transcendentals=0),
        name=name,
    )(*args, *after)


def hold(value, *after):
    return pl.pallas_call(
        lambda *refs: None,
        out_shape=jax.ShapeDtypeStruct(value.shape, value.dtype),
        in_specs=[pl.BlockSpec(memory_space=pl.ANY)] * (1 + len(after)),
        out_specs=pl.BlockSpec(memory_space=pl.ANY),
        input_output_aliases={0: 0},
        name="hold",
    )(value, *after)


def back_sum_body(cap, *refs):
    terms, out = refs[:-1], refs[-1]
    width = out.shape[2]
    total = terms[0][...].astype(F32)
    for ref in terms[1:]:
        total = total + ref[...].astype(F32)
    for z in range(out.shape[0]):
        y = total[z * cap : (z + 1) * cap, width:]
        out[z] = jnp.concatenate([total[:, :width], y], axis=0).astype(BF16)


def add_pair(near, far):
    got = swap(far, "ctx", 1)
    return [
        (near[j].astype(F32) + got[j].astype(F32)).astype(BF16) for j in range(near.shape[0])
    ]


def send_direct(both):
    return [both[0]] + [swap(block, "ctx", 2 * j) for j, block in enumerate(both) if j > 0]


def rms_scale(values):
    return lax.rsqrt(jnp.mean(values * values, axis=-1, keepdims=True) + EPS)


def iota(shape, axis):
    return lax.broadcasted_iota(jnp.int32, shape, axis)


def block_before(rows, tok, quarter):
    early, late = iota((rows, rows), 0), iota((rows, rows), 1)
    same = (early % tok) // quarter == (late % tok) // quarter
    return jnp.where(same & (early < late), 1.0, 0.0).astype(BF16)


def slot_hot(route0, route1, expert, before, tok, quarter, cap, parts):
    rows = route0.shape[1]
    named = (route0 == expert) | (route1 == expert)
    flags = jnp.broadcast_to(jnp.where(named, 1.0, 0.0), (16, rows)).astype(BF16)
    rank = nn(flags, before)[0:1].astype(jnp.int32)
    block = (iota((1, rows), 1) % tok) // quarter
    place = jnp.where(named, block * cap + rank, -1)
    return iota((parts * cap, rows), 0) == place, named


def pack_body(folded, wo, cot, info, x, *refs):
    weights, (out, message) = refs[:-2], refs[-2:]
    quarter, shard = cot.shape[0], wo.shape[1]
    width = cot.shape[2]
    tok = x.shape[0]
    wide = x[...].astype(F32)
    for s in range(2):
        message[s * tok : (s + 1) * tok, :] = wide[:, s, :].astype(BF16)
    if folded:
        rest = shard - folded
        cols = 3 * wo.shape[0]
        side = jnp.concatenate([w[folded:, :] for w in weights], axis=0)
        side = jnp.concatenate(
            [side, jnp.zeros((folded - 3 * rest, side.shape[1]), BF16)], axis=0
        )
        message[2 * tok :, :] = jnp.concatenate([w[:folded, :] for w in weights] + [side], axis=1)
    third = width // 3
    rows = 2 * quarter
    out[...] = jnp.zeros(out.shape, BF16)
    first = out.at[0]
    flat = cot[...].astype(F32)
    for s in range(2):
        piece = flat[:, s, :].astype(BF16)
        for c in range(3):
            lead = c * rows + s * quarter
            first[lead : lead + quarter, :third] = piece[:, c * third : (c + 1) * third]
    eye = (iota((shard, shard), 0) == iota((shard, shard), 1)).astype(F32).astype(BF16)
    first[:shard, third:] = nt(eye, wo[...]).astype(BF16)
    values = info[...]
    hi = values.astype(BF16).astype(F32)
    mid = (values - hi).astype(BF16).astype(F32)
    low = values - hi - mid
    total = jnp.zeros((16, LANES), F32)
    for s in range(2):
        terms = [term[:, 4 * s : 4 * s + 4] for term in (hi, mid, low)]
        stacked = jnp.concatenate(terms + [jnp.zeros((quarter, 4), F32)], axis=1).astype(BF16)
        spot = iota((quarter, LANES), 0) + s * quarter == iota((quarter, LANES), 1)
        total = total + tn(stacked, jnp.where(spot, 1.0, 0.0).astype(BF16))
    first[out.shape[1] - 16 :, :LANES] = total.astype(BF16)
    for z in range(1, out.shape[0]):
        out[z] = first[...]


def sent_body(hidden, gate, up, out):
    for c in range(out.shape[0]):
        out[c, :, :hidden] = gate[:, c * hidden : (c + 1) * hidden]
        out[c, :, hidden:] = up[:, c * hidden : (c + 1) * hidden]


def early_body(tok, quarter, *refs):
    pieces, cot_out, info_out, mats_out = refs
    exp_pos = lax.axis_index("exp")
    parts = pieces.shape[0]
    rows = 2 * tok
    third = cot_out.shape[1] // 3
    shard = mats_out.shape[0]
    info = jnp.zeros((16, rows), F32)
    for z in range(parts):
        for s in range(2):
            spot = s * tok + z * quarter
            for c in range(3):
                lead = c * 2 * quarter + s * quarter
                cot_out[spot : spot + quarter, c * third : (c + 1) * third] = pieces[
                    z, lead : lead + quarter, :third
                ]
        lane, row = iota((LANES, rows), 0), iota((LANES, rows), 1)
        target = (lane // quarter) * tok + z * quarter + lane % quarter
        spot = jnp.where((target == row) & (lane < 2 * quarter), 1.0, 0.0).astype(BF16)
        info = info + nn(pieces[z, pieces.shape[1] - 16 :, :LANES], spot)
    mats_out[...] = jnp.concatenate(
        [pieces[exp_pos ^ d, :shard, third:] for d in range(parts)], axis=1
    )
    low = info[0:4] + (info[4:8] + info[8:12])
    info_out[...] = jnp.concatenate([low, jnp.zeros((4, rows), F32)], axis=0)


def lay_rows(refs, out):
    if len(refs) == 1:
        out[...] = refs[0][...]
        return
    ctx_pos = lax.axis_index("ctx")
    for ref, i, d in each_block(refs):
        rows = ref.shape[1]
        out[pl.ds(pl.multiple_of((ctx_pos ^ d) * rows, rows), rows), :] = ref[i]


def lay_body(*refs):
    blocks, (mats_out, own_out) = refs[:-2], refs[-2:]
    lay_rows(blocks, mats_out)
    own_out[...] = mats_out[:, : own_out.shape[1]]


def project_body(hl, tok, folded, gain, *refs):
    q_out, kv_out, a_out, w = refs[-4:]
    blocks = refs[:-4]
    ctx_pos = lax.axis_index("ctx")
    rows = 2 * tok
    if folded:
        listed = each_block(blocks)
        for ref, i, d in listed:
            shard = w.shape[0] // len(listed)
            rest = shard - folded
            lead = (ctx_pos ^ d) * shard
            w[pl.ds(pl.multiple_of(lead, 16), folded), :] = ref[i, rows:, : 3 * hl]
            side = ref[i, rows:, 3 * hl :]
            w[pl.ds(pl.multiple_of(lead + folded, 16), rest), :] = jnp.concatenate(
                [side[t * rest : (t + 1) * rest] for t in range(3)], axis=1
            )
    else:
        w[...] = blocks[-1][...]
        blocks = blocks[:-1]
    listed = each_block(blocks)
    for lead in range(0, len(listed), 4):
        group = listed[lead : lead + 4]
        x = jnp.concatenate([ref[i, :rows, :] for ref, i, _ in group], axis=0).astype(F32)
        normed = (x * rms_scale(x) * gain[...]).astype(BF16)
        full = nn(normed, w[...] if lead == 0 else w[:, hl:]).astype(BF16)
        if lead == 0:
            a_out[...] = normed[:rows]
            q_out[...] = full[:rows, :hl]
            full = full[:, hl:]
        for t, (_, _, d) in enumerate(group):
            kv_out[ctx_pos ^ d] = full[t * rows : (t + 1) * rows].reshape(2, tok, 2 * hl)


def fold_lanes(value):
    rows, cols = value.shape
    if cols % LANES != LANES // 2:
        return value
    whole = [value[:, c : c + LANES] for c in range(0, cols - LANES // 2, LANES)]
    tail = value[:, cols - LANES // 2 :]
    tail = jnp.concatenate([tail[: rows // 2], tail[rows // 2 :]], axis=1)
    return jnp.concatenate(whole + [tail], axis=0)


def unfold_lanes(value, rows, cols):
    if cols % LANES != LANES // 2:
        return value
    count = cols // LANES
    whole = [value[c * rows : (c + 1) * rows] for c in range(count)]
    tail = value[count * rows :]
    tail = jnp.concatenate([tail[:, : LANES // 2], tail[:, LANES // 2 :]], axis=0)
    return jnp.concatenate(whole + [tail], axis=1)


def attend_body(heads, q, table, rev, kv_out, o_out, low_out, p_out):
    ctx_pos, exp_pos = lax.axis_index("ctx"), lax.axis_index("exp")
    rows = q.shape[0]
    tok = rows // 2
    hl = heads * HD
    seq_len = rev.shape[1]
    start = ctx_pos * tok
    buckets, head_total = table.shape
    pick = jnp.where(
        iota((8, head_total), 1) == exp_pos * heads + iota((8, head_total), 0), 1.0, 0.0
    )
    own_table = nt(pick, table[...], HIGH)
    hot = jnp.where(iota((buckets, seq_len), 0) == rev[...], 1.0, 0.0)
    bias = pltpu.roll(nn(own_table, hot, HIGH), start + 1, 1)
    open_keys = iota((tok, seq_len), 1) <= start + iota((tok, seq_len), 0)
    skewed = []
    for h in range(heads):
        wide = jnp.broadcast_to(bias[h : h + 1, :], (tok, seq_len))
        turned = pltpu.roll(wide, 0, 1, stride=1, stride_axis=0)
        skewed.append(jnp.where(open_keys, turned, FLOOR))
    halves = []
    for s in range(2):
        outs = []
        for h in range(heads):
            query = q[s * tok : (s + 1) * tok, h * HD : (h + 1) * HD]
            key = kv_out[:, s, :, h * HD : (h + 1) * HD].reshape(seq_len, HD)
            value = kv_out[:, s, :, hl + h * HD : hl + (h + 1) * HD].reshape(seq_len, HD)
            scores = nt(query, key) * (HD**-0.5) + skewed[h]
            top = jnp.max(scores, axis=-1, keepdims=True)
            weights = jnp.exp(scores - top)
            probs = weights * (1.0 / jnp.sum(weights, axis=-1, keepdims=True))
            p_out[s * heads + h] = probs
            outs.append(nn(probs.astype(BF16), value))
        out = jnp.concatenate(outs, axis=1)
        o_out[s * tok : (s + 1) * tok, :] = out
        halves.append(out.astype(BF16))
    packed = fold_lanes(jnp.concatenate(halves, axis=0))
    low_out[...] = packed


def gate_values(logits, info):
    route0, route1 = info[0:1].astype(jnp.int32), info[1:2].astype(jnp.int32)
    choice0 = jnp.zeros_like(info[0:1])
    choice1 = jnp.zeros_like(info[0:1])
    for e in range(logits.shape[0]):
        choice0 = choice0 + jnp.where(route0 == e, logits[e : e + 1], 0.0)
        choice1 = choice1 + jnp.where(route1 == e, logits[e : e + 1], 0.0)
    top = jnp.maximum(choice0, choice1)
    up0, up1 = jnp.exp(choice0 - top), jnp.exp(choice1 - top)
    total = up0 + up1
    return up0 / total, up1 / total


def route_body(tok, quarter, cap, parts, *refs):
    x, mats = refs[:2]
    lows = refs[2 : 2 + parts]
    gain, router_t, info_ref, cot, resid_out, gates_out, slots_out = refs[2 + parts :]
    exp_pos = lax.axis_index("exp")
    rows, width = 2 * tok, gain.shape[1]
    attn = nt(
        jnp.concatenate(
            [unfold_lanes(low[...], rows, mats.shape[1] // parts) for low in lows], axis=1
        ),
        mats[...],
    )
    for s in range(2):
        resid_out[s * tok : (s + 1) * tok, :] = (
            x[s * tok : (s + 1) * tok, :].astype(F32) + attn[s * tok : (s + 1) * tok]
        )
    resid = resid_out[...]
    normed = (resid * rms_scale(resid) * gain[...]).astype(BF16)
    logits = nt(router_t[...], normed.astype(F32), HIGH)
    info = info_ref[...]
    soft0, soft1 = gate_values(logits, info)
    gate0, gate1 = info[2:3] * soft0, info[3:4] * soft1
    gates_out[...] = jnp.concatenate([gate0, gate1, jnp.zeros((6, rows), F32)], axis=0)
    route0, route1 = info[0:1].astype(jnp.int32), info[1:2].astype(jnp.int32)
    before = block_before(rows, tok, quarter)
    hot, _ = slot_hot(route0, route1, exp_pos, before, tok, quarter, cap, parts)
    hot = jnp.where(hot, 1.0, 0.0).astype(BF16)
    first = route0 == exp_pos
    gate = jnp.where(first, gate0, gate1)
    slope = soft0 * soft1 * jnp.where(first, info[2:3], info[3:4])
    other = jnp.where(first, info[1:2], info[0:1])
    gate_hi, slope_hi = gate.astype(BF16).astype(F32), slope.astype(BF16).astype(F32)
    extras = jnp.concatenate(
        [gate_hi, gate - gate_hi, slope_hi, slope - slope_hi, other, jnp.zeros((LANES - 5, rows), F32)],
        axis=0,
    ).astype(BF16)
    slots_out[:, :width] = nn(hot, normed).astype(BF16)
    slots_out[:, width : width + LANES] = nt(hot, extras).astype(BF16)
    slots_out[:, width + LANES :] = nn(hot, cot[...]).astype(BF16)


def expert_back_body(count, *refs):
    xs = refs[:count]
    w_in, down, router_t, near_out, far_out, hid, dg_out, du_out, spread_out = refs[count:]
    exp_pos = lax.axis_index("exp")
    width, hidden = w_in.shape[0], down.shape[0]
    experts = router_t.shape[0]
    gate_w, up_w = w_in[:, :hidden], w_in[:, hidden:]
    down_w = down[...]
    done = 0
    side = near_out.shape[0]
    for x_group in grouped(xs):
        rows = stack(x_group, cols=slice(0, width))
        extras = stack(x_group, cols=slice(width, width + LANES)).astype(F32)
        step = rows.shape[0]
        part = slice(done, done + step)
        done = done + step
        gate = extras[:, 0:1] + extras[:, 1:2]
        slope = extras[:, 2:3] + extras[:, 3:4]
        other = extras[:, 4:5].astype(jnp.int32)
        pre = nn(rows, gate_w)
        up = nn(rows, up_w)
        raw = nt(stack(x_group, cols=slice(width + LANES, None)), down_w)
        squared = pre * pre
        tanh = jnp.tanh(GELU_C * (pre + GELU_A * pre * squared))
        half = 0.5 * (1.0 + tanh)
        act = pre * half
        hidden_low = (act * up).astype(BF16)
        hid[part, :] = hidden_low
        slope_act = half + 0.5 * pre * (1.0 - tanh * tanh) * (
            GELU_C * (1.0 + 3.0 * GELU_A * squared)
        )
        gate_grad = jnp.sum(hidden_low.astype(F32) * raw, axis=-1, keepdims=True)
        grad = gate * raw
        dg = (grad * up * slope_act).astype(BF16)
        du = (grad * act).astype(BF16)
        dg_out[part, :] = dg
        du_out[part, :] = du
        tilt = gate_grad * slope
        kind = iota((step, 8), 1)
        spread = jnp.where(kind == exp_pos, tilt, 0.0) - jnp.where(kind == other, tilt, 0.0)
        spread_out[part, :] = spread
        back = nt(dg, gate_w) + nt(du, up_w)
        for e in range(experts):
            back = back + spread[:, e : e + 1] * router_t[e : e + 1, :]
        out, lead = (near_out, done - step) if done <= side else (far_out, done - step - side)
        out[lead : lead + step, :width] = back.astype(BF16)
        out[lead : lead + step, width:] = nn(hidden_low, down_w).astype(BF16)


def expert_weights_body(count, *refs):
    xs = refs[:count]
    dg, du, *w_outs, wide = refs[count:]
    width = wide.shape[0] * wide.shape[1]
    gate_sum, up_sum = 0.0, 0.0
    done = 0
    for x_group in grouped(xs):
        rows = stack(x_group, cols=slice(0, width))
        part = slice(done, done + rows.shape[0])
        done = done + rows.shape[0]
        gate_sum = gate_sum + tn(rows, dg[part, :])
        up_sum = up_sum + tn(rows, du[part, :])
    w_grad = jnp.concatenate([gate_sum.astype(BF16), up_sum.astype(BF16)], axis=1)
    if len(w_outs) == 1:
        w_outs[0][...] = w_grad.reshape(w_outs[0].shape)
        return
    ctx_pos = lax.axis_index("ctx")
    wide[...] = w_grad.reshape(wide.shape)
    for d, out in enumerate(w_outs):
        out[...] = wide[ctx_pos ^ d]


def expert_rest_body(count, *refs):
    xs = refs[:count]
    hid, spread, down_out, router_out = refs[count:]
    width = down_out.shape[1]
    down_sum, router_sum = 0.0, 0.0
    done = 0
    for x_group in grouped(xs):
        rows = stack(x_group, cols=slice(0, width))
        extras = stack(x_group, cols=slice(width, width + LANES)).astype(F32)
        part = slice(done, done + rows.shape[0])
        done = done + rows.shape[0]
        gate = extras[:, 0:1] + extras[:, 1:2]
        cot = stack(x_group, cols=slice(width + LANES, None))
        dy = (gate * cot.astype(F32)).astype(BF16)
        down_sum = down_sum + tn(hid[part, :], dy)
        router_sum = router_sum + tn(spread[part, :], rows.astype(F32), HIGH)
    down_out[...] = down_sum
    router_out[...] = router_sum


def widen_body(*refs):
    blocks, (gate_out, up_out) = refs[:-2], refs[-2:]
    hidden = blocks[0].shape[-1] // 2
    if len(blocks) == 1:
        for c in range(blocks[0].shape[0]):
            gate_out[:, c * hidden : (c + 1) * hidden] = blocks[0][c, :, :hidden].astype(F32)
            up_out[:, c * hidden : (c + 1) * hidden] = blocks[0][c, :, hidden:].astype(F32)
        return
    ctx_pos = lax.axis_index("ctx")
    for d, block in enumerate(blocks):
        spot = pl.ds(pl.multiple_of((ctx_pos ^ d) * hidden, LANES), hidden)
        gate_out[:, spot] = block[:, :hidden].astype(F32)
        up_out[:, spot] = block[:, hidden:].astype(F32)


def mix_body(tok, quarter, cap, parts, resid, info_ref, gates_ref, ys, out, held, wide):
    exp_pos = lax.axis_index("exp")
    rows, width = 2 * tok, resid.shape[1]
    info, gates = info_ref[...], gates_ref[...]
    route0, route1 = info[0:1].astype(jnp.int32), info[1:2].astype(jnp.int32)
    before = block_before(rows, tok, quarter)
    block = (iota((1, rows), 1) % tok) // quarter
    weights = []
    for e in range(parts):
        named = ((route0 == e) | (route1 == e)) & (block == exp_pos)
        flags = jnp.broadcast_to(jnp.where(named, 1.0, 0.0), (16, rows)).astype(BF16)
        rank = jnp.where(named, nn(flags, before)[0:1].astype(jnp.int32), -1)
        gate = jnp.where(route0 == e, gates[0:1], gates[1:2])
        weights.append(jnp.where(iota((cap, rows), 0) == rank, gate, 0.0))
    weights = jnp.concatenate(weights, axis=0)
    hi = weights.astype(BF16)
    low = (weights - hi.astype(F32)).astype(BF16)
    y = jnp.concatenate(
        [ys[e].astype(F32)[parts * cap :] for e in range(parts)], axis=0
    ).astype(BF16)
    held[...] = resid[...] + tn(hi, y) + tn(low, y)
    for s in range(2):
        spot = pl.ds(pl.multiple_of(s * tok + exp_pos * quarter, quarter), quarter)
        wide[:, s, :] = held[spot, :]
    out[...] = wide[...].astype(BF16)


def attend_back_body(heads, tok, quarter, cap, parts, *refs):
    (
        returned, resid_ref, cot, gain, info_ref, o, out_t, q, kv, p,
        own_out, dq_out, near_out, far_out, grad_out, sums_out, small_out, held, dkv,
    ) = refs
    ctx_pos, exp_pos = lax.axis_index("ctx"), lax.axis_index("exp")
    rows, width = resid_ref.shape
    hl = heads * HD
    count = kv.shape[0]
    seq_len = count * tok
    start = ctx_pos * tok
    info = info_ref[...]
    route0, route1 = info[0:1].astype(jnp.int32), info[1:2].astype(jnp.int32)
    before = block_before(rows, tok, quarter)
    grad = jnp.zeros((rows, width), F32)
    for e in range(parts):
        hot, _ = slot_hot(route0, route1, e, before, tok, quarter, cap, parts)
        piece = returned[e].astype(F32)[: parts * cap].astype(BF16)
        grad = grad + tn(jnp.where(hot, 1.0, 0.0).astype(BF16), piece)
    resid = resid_ref[...]
    scale = rms_scale(resid)
    centred = resid * scale
    small_out[...] = jnp.broadcast_to(
        jnp.sum(grad * centred, axis=0, keepdims=True) * (1.0 / parts), small_out.shape
    )
    inner = grad * gain[...]
    held[...] = cot[...].astype(F32) + scale * (
        inner - centred * jnp.mean(inner * centred, axis=-1, keepdims=True)
    )
    for s in range(2):
        spot = pl.ds(pl.multiple_of(s * tok + exp_pos * quarter, quarter), quarter)
        own_out[s * quarter : (s + 1) * quarter, :] = held[spot, :]
    attn_grad = held[...].astype(BF16)
    grad_o = nn(attn_grad, out_t[...]).astype(BF16)
    grad_out[...] = attn_grad
    sums = [jnp.zeros((tok, seq_len), F32) for _ in range(heads)]
    for s in range(2):
        here = slice(s * tok, (s + 1) * tok)
        keys, values, queries = [], [], []
        for h in range(heads):
            cols = slice(h * HD, (h + 1) * HD)
            probs = p[s * heads + h]
            key = kv[:, s, :, cols].reshape(seq_len, HD)
            value = kv[:, s, :, hl + h * HD : hl + (h + 1) * HD].reshape(seq_len, HD)
            do = grad_o[here, cols]
            delta = jnp.sum(do.astype(F32) * o[here, cols], axis=-1, keepdims=True)
            ds = (probs * (nt(do, value) - delta)).astype(BF16)
            sums[h] = sums[h] + ds.astype(F32)
            values.append(tn(probs.astype(BF16), do).astype(BF16))
            keys.append((tn(ds, q[here, cols]) * (HD**-0.5)).astype(BF16))
            queries.append(nn(ds, key) * (HD**-0.5))
        dq_out[here, :] = jnp.concatenate(queries, axis=1).astype(BF16)
        dkv[:, s] = jnp.concatenate(keys + values, axis=1).reshape(count, tok, 2 * hl)
    for j in range(count // 2):
        near_out[j] = dkv[ctx_pos ^ (2 * j)].reshape(rows, 2 * hl)
        far_out[j] = dkv[ctx_pos ^ (2 * j + 1)].reshape(rows, 2 * hl)
    for h in range(heads):
        sums_out[h] = sums[h]


def table_body(buckets, sums, attn_grad, low, rev, table_out, dout_t):
    ctx_pos, exp_pos = lax.axis_index("ctx"), lax.axis_index("exp")
    heads, tok, seq_len = sums.shape
    width = table_out.shape[1]
    start = ctx_pos * tok
    dout_t[...] = tn(
        attn_grad[...], unfold_lanes(low[...], attn_grad.shape[0], dout_t.shape[1])
    ).astype(BF16)
    lines = []
    for h in range(heads):
        turned = sums[h]
        step = 1
        while step < tok:
            bit = (iota((tok, seq_len), 0) // step) % 2 == 1
            turned = jnp.where(bit, pltpu.roll(turned, seq_len - step, 1), turned)
            step *= 2
        lines.append(jnp.sum(turned, axis=0, keepdims=True))
    lines = jnp.concatenate(lines + [jnp.zeros((8 - heads, seq_len), F32)], axis=0)
    lines = pltpu.roll(lines, seq_len - start - 1, 1)
    counts = jnp.zeros((8, LANES), F32)
    for lead in range(0, seq_len, 512):
        cut = slice(lead, min(lead + 512, seq_len))
        here = lines[:, cut]
        hot = jnp.where(iota((here.shape[1], LANES), 1) == rev[cut, :], 1.0, 0.0)
        counts = counts + nn(here, hot, HIGH)
    table = jnp.zeros((8, width), F32)
    for h in range(heads):
        spot = (exp_pos * heads + h) * buckets
        place = jnp.where(
            (iota((LANES, width), 1) == spot + iota((LANES, width), 0))
            & (iota((LANES, width), 0) < buckets),
            1.0,
            0.0,
        )
        table = table + nn(jnp.broadcast_to(counts[h : h + 1], (8, LANES)), place, HIGH)
    table_out[...] = table


def back_project_body(quarter, parts, *refs):
    da_out, w_near, w_far, small_out, wide = refs[-5:]
    dq, w, a, dout_t, x, gain, small, table, router = refs[:9]
    terms = refs[9:-5]
    ctx_pos, exp_pos = lax.axis_index("ctx"), lax.axis_index("exp")
    rows, width = a.shape
    tok = rows // 2
    dkv = terms[0][...].astype(F32)
    for term in terms[1:]:
        dkv = dkv + term[...].astype(F32)
    grads = jnp.concatenate([dq[...], dkv.astype(BF16)], axis=1)
    da = nt(grads, w[...])
    total = jnp.zeros((1, width), F32)
    for s in range(2):
        piece = x[s * tok : (s + 1) * tok, :].astype(F32)
        here = da[s * tok : (s + 1) * tok]
        total = total + jnp.sum(piece * rms_scale(piece) * here, axis=0, keepdims=True)
        for z in range(parts):
            da_out[z, s * quarter : (s + 1) * quarter, :] = here[
                z * quarter : (z + 1) * quarter
            ].astype(BF16)
    small_out[0:1, :] = total
    small_out[1:2, :] = small[0:1, :]
    small_out[2:3, :] = table[0:1, :]
    small_out[3:7, :] = router[0:4, :]
    small_out[7:8, :] = jnp.zeros((1, width), F32)
    full = jnp.concatenate([tn(a[...], grads).astype(BF16), dout_t[...]], axis=1)
    if len(wide.shape) == 2:
        wide[...] = full
        w_near[...] = full
        w_far[...] = full
        return
    count, shard, _ = wide.shape
    wide[...] = full.reshape(wide.shape)
    for j in range(count // 2):
        w_near[j] = wide[ctx_pos ^ (2 * j)]
        w_far[j] = wide[ctx_pos ^ (2 * j + 1)]


def finish_body(tok, quarter, x, gain, own, pieces, out):
    exp_pos = lax.axis_index("exp")
    width = gain.shape[1]
    for s in range(2):
        spot = pl.ds(pl.multiple_of(s * tok + exp_pos * quarter, quarter), quarter)
        rows = x[spot, :].astype(F32)
        here = slice(s * quarter, (s + 1) * quarter)
        grad = pieces[0, here, :].astype(F32)
        for z in range(1, pieces.shape[0]):
            grad = grad + pieces[z, here, :].astype(F32)
        scale = rms_scale(rows)
        centred = rows * scale
        inner = grad * gain[...]
        out[:, s, :] = own[here, :] + scale * (
            inner - centred * jnp.mean(inner * centred, axis=-1, keepdims=True)
        )


def last_body(count, tok, quarter, x, gain, own, pieces, *refs):
    terms, smalls = refs[:count], refs[count:-9]
    finish_out, q_out, k_out, v_out, o_out, attn_out, ffn_out, table_out, router_out = refs[-9:]
    finish_body(tok, quarter, x, gain, own, pieces, finish_out)
    hl = q_out.shape[1]
    total = terms[0][...].astype(F32)
    for term in terms[1:]:
        total = total + term[...].astype(F32)
    q_out[...] = total[:, :hl]
    k_out[...] = total[:, hl : 2 * hl]
    v_out[...] = total[:, 2 * hl : 3 * hl]
    o_out[...] = total[:, 3 * hl :].T
    small = smalls[0][...]
    for term in smalls[1:]:
        small = small + term[...]
    attn_out[...] = small[0]
    ffn_out[...] = small[1]
    heads, buckets = table_out.shape
    for h in range(heads):
        table_out[h : h + 1, :] = small[2:3, h * buckets : (h + 1) * buckets]
    router_out[...] = small[3 : 3 + router_out.shape[0], :]


def on_device(
    block_input,
    output_cotangent,
    attn_gain,
    query_weight,
    key_weight,
    value_weight,
    output_weight,
    bias_table,
    buckets,
    ffn_gain,
    router_weight,
    routes,
    route_prior,
    gate_weight,
    up_weight,
    down_weight,
):
    tok, seqs, width = block_input.shape
    quarter = routes.shape[0]
    ctx_size, parts = lax.axis_size("ctx"), lax.axis_size("exp")
    hl = query_weight.shape[1]
    heads = hl // HD
    cap = (3 * quarter * seqs + 3) // 4
    slots = parts * cap
    rows = tok * seqs
    shard = query_weight.shape[0]
    hidden = down_weight.shape[1]
    half = ctx_size // 2
    seq_len = tok * ctx_size
    aligned = shard % 16 == 0
    gain_one, gain_two = attn_gain.reshape(1, width), ffn_gain.reshape(1, width)
    router_t = router_weight.T
    rev = buckets[::-1].reshape(1, seq_len)
    down = down_weight.reshape(hidden, width)

    folded = shard * 5 // 6 if shard % 96 == 0 else 0
    info = jnp.concatenate([routes.astype(F32), route_prior], axis=2).reshape(quarter, 4 * seqs)
    cot_pack, x = call(
        functools.partial(pack_body, folded),
        "pack",
        [
            ((parts, max(3 * seqs * quarter, shard) + 16, width // 3 + hl), BF16),
            ((rows + folded, width), BF16),
        ],
        output_weight, output_cotangent, info, block_input,
        *([query_weight, key_weight, value_weight] if folded else []), us=1.5, wide=True,
    )
    x_blocks = gather_ctx(x)
    if not folded:
        packed = jnp.concatenate([query_weight, key_weight, value_weight], axis=1)
        x_blocks = x_blocks + [lax.all_gather(packed, "ctx", axis=0, tiled=True)]
    cot_packs = trade_exp(cot_pack)
    cot_block, info_block, mats = call(
        functools.partial(early_body, tok, quarter),
        "early_slots",
        [
            ((rows, width), BF16),
            ((8, rows), F32),
            ((shard, parts * hl), BF16),
        ],
        cot_packs,
    )
    q, kv_all, normed, w_qkv = call(
        functools.partial(project_body, hl, tok, folded),
        "project",
        [
            ((rows, hl), BF16),
            ((ctx_size, seqs, tok, 2 * hl), BF16),
            ((rows, width), BF16),
            ((width, 3 * hl), BF16),
        ],
        gain_one, *x_blocks, us=4.0, after=[info_block], wide=True,
    )
    mats_blocks = (
        gather_ctx(mats, [q]) if aligned else [lax.all_gather(mats, "ctx", axis=0, tiled=True)]
    )

    sent = call(
        functools.partial(sent_body, hidden),
        "sent",
        ((ctx_size, shard, 2 * hidden), BF16),
        gate_weight.reshape(shard, ctx_size * hidden), up_weight.reshape(shard, ctx_size * hidden),
        us=2.0, after=[q],
    )
    mats_full, out_t, laid = call(
        lay_body, "lay_out", [((width, parts * hl), BF16), ((width, hl), BF16)], *mats_blocks,
        us=2.5, token=True,
    )
    low_shape = (rows * hl // LANES, LANES) if hl % LANES == LANES // 2 else (rows, hl)
    o, low, p = call(
        functools.partial(attend_body, heads),
        "attend",
        [
            ((rows, hl), F32),
            (low_shape, BF16),
            ((seqs * heads, tok, seq_len), F32),
        ],
        q, bias_table, rev, kv_all, us=4.8, after=[laid], wide=True,
    )
    lows = spread_exp(low)
    w_in = lax.all_to_all(hold(sent, low), "ctx", split_axis=0, concat_axis=0, tiled=True)
    w_in = w_in.reshape(width, 2 * hidden)

    resid, gates, x_slots = call(
        functools.partial(route_body, tok, quarter, cap, parts),
        "route",
        [((rows, width), F32), ((8, rows), F32), ((slots, 2 * width + LANES), BF16)],
        x, mats_full, *lows, gain_two, router_t, info_block, cot_block, us=3.7,
    )
    x_blocks = gather_ctx(x_slots)
    side = half * slots
    cut = len(x_blocks)
    back_near, back_far, hid, dg, du, spread = call(
        functools.partial(expert_back_body, cut),
        "expert_back",
        [((side, 2 * width), BF16)] * 2 + [((2 * side, hidden), BF16)] * 3 + [((2 * side, 8), F32)],
        *x_blocks, w_in, down, router_t, us=8.0, wide=True,
    )
    back_terms = send_direct(
        add_pair(
            back_near.reshape(half, slots, 2 * width), back_far.reshape(half, slots, 2 * width)
        )
    )
    back_sums, summed = call(
        functools.partial(back_sum_body, cap),
        "sum_back",
        ((parts, slots + cap, width), BF16),
        *back_terms, us=2.0, token=True,
    )
    returned = trade_exp(back_sums)
    by_permutes = ctx_size <= 8 and hidden % LANES == 0
    w_shape = (shard, 2 * hidden)
    *w_grads, weighed = call(
        functools.partial(expert_weights_body, cut),
        "expert_weights",
        [(w_shape, BF16)] * ctx_size if by_permutes else [((ctx_size, *w_shape), BF16)],
        *x_blocks, dg, du, us=4.0, after=[summed], wide=True, token=True,
        scratch=[pltpu.VMEM((ctx_size, *w_shape), BF16)],
    )
    down_grad, router = call(
        functools.partial(expert_rest_body, cut),
        "expert_rest",
        [((hidden, width), F32), ((8, width), F32)],
        *x_blocks, hid, spread, us=3.0, after=[weighed], wide=True,
    )
    if by_permutes:
        w_back = [w_grads[0]] + [swap(w_grads[d], "ctx", d) for d in range(1, ctx_size)]
    else:
        w_back = [lax.all_to_all(w_grads[0], "ctx", split_axis=0, concat_axis=0, tiled=True)]
    gate_grad, up_grad, widened = call(
        widen_body,
        "widen",
        [((shard, ctx_size * hidden), F32)] * 2,
        *w_back, us=2.0, token=True,
    )
    resid_grad, dq, dkv_near, dkv_far, attn_grad, score_sums, small = call(
        functools.partial(attend_back_body, heads, tok, quarter, cap, parts),
        "attend_back",
        [
            ((seqs * quarter, width), F32),
            ((rows, hl), BF16),
            ((half, rows, 2 * hl), BF16),
            ((half, rows, 2 * hl), BF16),
            ((rows, width), BF16),
            ((heads, tok, seq_len), F32),
            ((8, width), F32),
        ],
        returned, resid, cot_block, gain_two, info_block, o, out_t, q, kv_all, p,
        us=8.0,
        scratch=[
            pltpu.VMEM((rows, width), F32),
            pltpu.VMEM((ctx_size, seqs, tok, 2 * hl), BF16),
        ],
        after=[widened, router], wide=True,
    )
    dkv_both = add_pair(dkv_near, dkv_far)
    dkv_terms = send_direct(dkv_both)
    block_output, mixed = call(
        functools.partial(mix_body, tok, quarter, cap, parts),
        "mix",
        ((quarter, seqs, width), BF16),
        resid, info_block, gates, returned,
        scratch=[pltpu.VMEM((rows, width), F32), pltpu.VMEM((quarter, seqs, width), F32)],
        token=True,
        after=[dkv_both[0]],
    )
    table, dout_t = call(
        functools.partial(table_body, bias_table.shape[0]),
        "table",
        [((8, width), F32), ((width, hl), BF16)],
        score_sums, attn_grad, low, rev.reshape(seq_len, 1), us=3.0, after=[dkv_both[0]],
    )
    w_shape = (half, shard, 4 * hl) if aligned else (width, 4 * hl)
    da_parts, w_near, w_far, small = call(
        functools.partial(back_project_body, quarter, parts),
        "back_project",
        [((parts, seqs * quarter, width), BF16)]
        + [(w_shape, BF16), (w_shape, BF16), ((8, width), F32)],
        dq, w_qkv, normed, dout_t, x, gain_one, small, table, router, *dkv_terms, us=3.4,
        scratch=[
            pltpu.VMEM((ctx_size, shard, 4 * hl) if aligned else (width, 4 * hl), BF16),
        ],
        after=[mixed],
    )
    da_terms = trade_exp(da_parts)
    if aligned:
        w_both = add_pair(w_near, w_far)
        w_terms = send_direct(w_both)
    else:
        w_terms = [lax.psum_scatter(w_near.astype(F32), "ctx", scatter_dimension=0, tiled=True)]
    small = sum(spread_exp(small))
    small = small + swap(small, "ctx", 1)
    smalls = [small] + [swap(small, "ctx", 2 * j) for j in range(1, half)]
    buckets_total, head_total = bias_table.shape
    (
        input_grad, query_grad, key_grad, value_grad, output_grad,
        attn_gain_grad, ffn_gain_grad, table_grad, router_grad,
    ) = call(
        functools.partial(last_body, len(w_terms), tok, quarter),
        "last",
        [((quarter, seqs, width), F32)] + [((shard, hl), F32)] * 3
        + [((hl, shard), F32), ((width,), F32), ((width,), F32)]
        + [((head_total, buckets_total), F32), ((router_t.shape[0], width), F32)],
        x, gain_one, resid_grad, da_terms, *w_terms, *smalls, us=2.5,
    )
    return (
        block_output,
        input_grad,
        attn_gain_grad,
        query_grad,
        key_grad,
        value_grad,
        output_grad,
        table_grad.T,
        ffn_gain_grad,
        router_grad.T,
        gate_grad[None],
        up_grad[None],
        down_grad.reshape(1, hidden, width),
    )


def solution(mesh):
    return jax.shard_map(
        on_device,
        mesh=mesh,
        in_specs=(
            P("ctx", None, None),
            P(("ctx", "exp"), None, None),
            P(),
            P("ctx", "exp"),
            P("ctx", "exp"),
            P("ctx", "exp"),
            P("exp", "ctx"),
            P(),
            P(),
            P(),
            P(),
            P(("ctx", "exp"), None, None),
            P(("ctx", "exp"), None, None),
            P("exp", "ctx", None),
            P("exp", "ctx", None),
            P("exp", "ctx", None),
        ),
        out_specs=(
            P(("ctx", "exp"), None, None),
            P(("ctx", "exp"), None, None),
            P(),
            P("ctx", "exp"),
            P("ctx", "exp"),
            P("ctx", "exp"),
            P("exp", "ctx"),
            P(),
            P(),
            P(),
            P("exp", "ctx", None),
            P("exp", "ctx", None),
            P("exp", "ctx", None),
        ),
        check_vma=False,
    )
```

```python
import functools

import jax
import jax.numpy as jnp
from jax import lax
from jax.experimental import pallas as pl
from jax.experimental.pallas import tpu as pltpu
from jax.sharding import PartitionSpec as P

HD = 64
EPS = 1e-06
FLOOR = -1e30
HIGH = lax.Precision.HIGHEST
F32 = jnp.float32
BF16 = jnp.bfloat16
LANES = 128
GELU_C = 0.7978845608028654
GELU_A = 0.044715


def swap(value, axis, bits):
    devices = lax.axis_size(axis)
    return lax.ppermute(value, axis, [(i, i ^ bits) for i in range(devices)])


def hold_with_token(value, *after):
    def body(*refs):
        refs[-1][...] = jnp.zeros(refs[-1].shape, F32)

    return pl.pallas_call(
        body,
        out_shape=[
            jax.ShapeDtypeStruct(value.shape, value.dtype),
            jax.ShapeDtypeStruct((8, LANES), F32),
        ],
        in_specs=[pl.BlockSpec(memory_space=pl.ANY)] * (1 + len(after)),
        out_specs=[pl.BlockSpec(memory_space=pl.ANY), pl.BlockSpec(memory_space=pltpu.VMEM)],
        input_output_aliases={0: 0},
        name="hold",
    )(value, *after)


def gather_ctx(value, after=()):
    devices = lax.axis_size("ctx")
    near = [value[None]] + [swap(value, "ctx", 2 * j)[None] for j in range(1, devices // 2)]
    tokens = []
    if after:
        held = [hold_with_token(block, *after) for block in near[1:]]
        near, tokens = near[:1] + [block for block, _ in held], [token for _, token in held]
    if devices > 8:
        near = [jnp.concatenate(near, axis=0)]
    blocks = near + [swap(block, "ctx", 1) for block in near]
    return (blocks, tokens) if after else blocks


def each_block(refs):
    half = sum(ref.shape[0] for ref in refs) // 2
    listed = [(ref, i) for ref in refs for i in range(ref.shape[0])]
    return [(ref, i, 2 * (t % half) + t // half) for t, (ref, i) in enumerate(listed)]


def grouped(refs):
    listed = [(ref, i) for ref in refs for i in range(ref.shape[0])]
    return [listed[t : t + 4] for t in range(0, len(listed), 4)]


def stack(group, rows=slice(None), cols=slice(None)):
    return jnp.concatenate([ref[i, rows, cols] for ref, i in group], axis=0)


def trade_exp(value):
    return lax.all_to_all(value, "exp", split_axis=0, concat_axis=0, tiled=True)


def spread_exp(value):
    return [value] + [swap(value, "exp", d) for d in range(1, lax.axis_size("exp"))]


def nn(left, right, precision=None):
    return lax.dot_general(
        left, right, (((1,), (0,)), ((), ())), precision=precision, preferred_element_type=F32
    )


def nt(left, right, precision=None):
    return lax.dot_general(
        left, right, (((1,), (1,)), ((), ())), precision=precision, preferred_element_type=F32
    )


def tn(left, right, precision=None):
    return lax.dot_general(
        left, right, (((0,), (0,)), ((), ())), precision=precision, preferred_element_type=F32
    )


def room(shape, dtype):
    *lead, rows, cols = (1, 1, *shape)
    size = jnp.dtype(dtype).itemsize
    tile = 32 // size
    total = -(-rows // tile) * tile * -(-cols // LANES) * LANES * size
    for extent in lead:
        total *= extent
    return total


def call(body, name, outs, *args, us=2.0, scratch=(), after=(), wide=False, token=False):
    single = not isinstance(outs, list)
    outs = ([outs] if single else outs) + ([((8, LANES), F32)] if token else [])
    single = len(outs) == 1
    specs = [pl.BlockSpec(memory_space=pltpu.VMEM)] * len(args)
    specs += [pl.BlockSpec(memory_space=pl.ANY)] * len(after)
    shapes = [jax.ShapeDtypeStruct(*o) for o in outs]
    out_specs = [pl.BlockSpec(memory_space=pltpu.VMEM)] * len(shapes)
    held = sum(room(a.shape, a.dtype) for a in (*args, *shapes))
    held += sum(room(a.shape, a.dtype) for a in scratch)
    limit = min(62 * 2**20, max(16 * 2**20 + 2 * held, 60 * 2**20 if wide else 0))

    def run(*refs):
        rest = refs[len(args) + len(after) :]
        if token:
            place = len(shapes) - 1
            rest[place][...] = jnp.zeros(rest[place].shape, F32)
            rest = rest[:place] + rest[place + 1 :]
        body(*refs[: len(args)], *rest)

    return pl.pallas_call(
        run,
        out_shape=shapes[0] if single else shapes,
        in_specs=specs,
        out_specs=out_specs[0] if single else out_specs,
        scratch_shapes=list(scratch),
        compiler_params=pltpu.CompilerParams(vmem_limit_bytes=limit),
        cost_estimate=pl.CostEstimate(flops=0, bytes_accessed=int(us * 3.0e4), transcendentals=0),
        name=name,
    )(*args, *after)


def hold(value, *after):
    return pl.pallas_call(
        lambda *refs: None,
        out_shape=jax.ShapeDtypeStruct(value.shape, value.dtype),
        in_specs=[pl.BlockSpec(memory_space=pl.ANY)] * (1 + len(after)),
        out_specs=pl.BlockSpec(memory_space=pl.ANY),
        input_output_aliases={0: 0},
        name="hold",
    )(value, *after)


def back_sum_body(cap, *refs):
    terms, out = refs[:-1], refs[-1]
    width = out.shape[2]
    total = terms[0][...].astype(F32)
    for ref in terms[1:]:
        total = total + ref[...].astype(F32)
    for z in range(out.shape[0]):
        y = total[z * cap : (z + 1) * cap, width:]
        out[z] = jnp.concatenate([total[:, :width], y], axis=0).astype(BF16)


def add_pair(near, far):
    got = swap(far, "ctx", 1)
    return [
        (near[j].astype(F32) + got[j].astype(F32)).astype(BF16) for j in range(near.shape[0])
    ]


def send_direct(both):
    return [both[0]] + [swap(block, "ctx", 2 * j) for j, block in enumerate(both) if j > 0]


def rms_scale(values):
    return lax.rsqrt(jnp.mean(values * values, axis=-1, keepdims=True) + EPS)


def iota(shape, axis):
    return lax.broadcasted_iota(jnp.int32, shape, axis)


def block_before(rows, tok, quarter):
    early, late = iota((rows, rows), 0), iota((rows, rows), 1)
    same = (early % tok) // quarter == (late % tok) // quarter
    return jnp.where(same & (early < late), 1.0, 0.0).astype(BF16)


def slot_hot(route0, route1, expert, before, tok, quarter, cap, parts):
    rows = route0.shape[1]
    named = (route0 == expert) | (route1 == expert)
    flags = jnp.broadcast_to(jnp.where(named, 1.0, 0.0), (16, rows)).astype(BF16)
    rank = nn(flags, before)[0:1].astype(jnp.int32)
    block = (iota((1, rows), 1) % tok) // quarter
    place = jnp.where(named, block * cap + rank, -1)
    return iota((parts * cap, rows), 0) == place, named


def pack_body(folded, wo, cot, info, x, *refs):
    weights, (out, message) = refs[:-2], refs[-2:]
    quarter, shard = cot.shape[0], wo.shape[1]
    width = cot.shape[2]
    tok = x.shape[0]
    wide = x[...].astype(F32)
    for s in range(2):
        message[s * tok : (s + 1) * tok, :] = wide[:, s, :].astype(BF16)
    if folded:
        rest = shard - folded
        cols = 3 * wo.shape[0]
        side = jnp.concatenate([w[folded:, :] for w in weights], axis=0)
        side = jnp.concatenate(
            [side, jnp.zeros((folded - 3 * rest, side.shape[1]), BF16)], axis=0
        )
        message[2 * tok :, :] = jnp.concatenate([w[:folded, :] for w in weights] + [side], axis=1)
    third = width // 3
    rows = 2 * quarter
    out[...] = jnp.zeros(out.shape, BF16)
    first = out.at[0]
    flat = cot[...].astype(F32)
    for s in range(2):
        piece = flat[:, s, :].astype(BF16)
        for c in range(3):
            lead = c * rows + s * quarter
            first[lead : lead + quarter, :third] = piece[:, c * third : (c + 1) * third]
    eye = (iota((shard, shard), 0) == iota((shard, shard), 1)).astype(F32).astype(BF16)
    first[:shard, third:] = nt(eye, wo[...]).astype(BF16)
    values = info[...]
    hi = values.astype(BF16).astype(F32)
    mid = (values - hi).astype(BF16).astype(F32)
    low = values - hi - mid
    total = jnp.zeros((16, LANES), F32)
    for s in range(2):
        terms = [term[:, 4 * s : 4 * s + 4] for term in (hi, mid, low)]
        stacked = jnp.concatenate(terms + [jnp.zeros((quarter, 4), F32)], axis=1).astype(BF16)
        spot = iota((quarter, LANES), 0) + s * quarter == iota((quarter, LANES), 1)
        total = total + tn(stacked, jnp.where(spot, 1.0, 0.0).astype(BF16))
    first[out.shape[1] - 16 :, :LANES] = total.astype(BF16)
    for z in range(1, out.shape[0]):
        out[z] = first[...]


def sent_body(hidden, gate, up, out):
    for c in range(out.shape[0]):
        out[c, :, :hidden] = gate[:, c * hidden : (c + 1) * hidden]
        out[c, :, hidden:] = up[:, c * hidden : (c + 1) * hidden]


def early_body(tok, quarter, cap, *refs):
    pieces, cot_out, info_out, both_out = refs
    exp_pos = lax.axis_index("exp")
    parts = pieces.shape[0]
    rows = 2 * tok
    third = cot_out.shape[1] // 3
    slots = parts * cap
    shard = both_out.shape[0] - slots
    info = jnp.zeros((16, rows), F32)
    for z in range(parts):
        for s in range(2):
            spot = s * tok + z * quarter
            for c in range(3):
                lead = c * 2 * quarter + s * quarter
                cot_out[spot : spot + quarter, c * third : (c + 1) * third] = pieces[
                    z, lead : lead + quarter, :third
                ]
        lane, row = iota((LANES, rows), 0), iota((LANES, rows), 1)
        target = (lane // quarter) * tok + z * quarter + lane % quarter
        spot = jnp.where((target == row) & (lane < 2 * quarter), 1.0, 0.0).astype(BF16)
        info = info + nn(pieces[z, pieces.shape[1] - 16 :, :LANES], spot)
    both_out[slots:, :] = jnp.concatenate(
        [pieces[exp_pos ^ d, :shard, third:] for d in range(parts)], axis=1
    )
    low = info[0:4] + (info[4:8] + info[8:12])
    info_out[...] = jnp.concatenate([low, jnp.zeros((4, rows), F32)], axis=0)
    before = block_before(rows, tok, quarter)
    route0, route1 = low[0:1].astype(jnp.int32), low[1:2].astype(jnp.int32)
    hot, _ = slot_hot(route0, route1, exp_pos, before, tok, quarter, cap, parts)
    both_out[:slots, :] = nn(jnp.where(hot, 1.0, 0.0).astype(BF16), cot_out[...]).astype(BF16)


def lay_rows(refs, out, lead=0):
    if len(refs) == 1:
        out[...] = refs[0][...]
        return
    ctx_pos = lax.axis_index("ctx")
    for ref, i, d in each_block(refs):
        rows = ref.shape[1] - lead
        out[pl.ds(pl.multiple_of((ctx_pos ^ d) * rows, rows), rows), :] = ref[i, lead:, :]


def lay_body(lead, *refs):
    blocks, (mats_out, own_out) = refs[:-2], refs[-2:]
    lay_rows(blocks, mats_out, lead)
    own_out[...] = mats_out[:, : own_out.shape[1]]


def fold_lanes(value):
    rows, cols = value.shape
    if cols % LANES != LANES // 2:
        return value
    whole = [value[:, c : c + LANES] for c in range(0, cols - LANES // 2, LANES)]
    tail = value[:, cols - LANES // 2 :]
    tail = jnp.concatenate([tail[: rows // 2], tail[rows // 2 :]], axis=1)
    return jnp.concatenate(whole + [tail], axis=0)


def unfold_lanes(value, rows, cols):
    if cols % LANES != LANES // 2:
        return value
    count = cols // LANES
    whole = [value[c * rows : (c + 1) * rows] for c in range(count)]
    tail = value[count * rows :]
    tail = jnp.concatenate([tail[:, : LANES // 2], tail[:, LANES // 2 :]], axis=0)
    return jnp.concatenate(whole + [tail], axis=1)


def project_body(hl, tok, folded, gain, *refs):
    q_out, kv_out, a_out, w = refs[-4:]
    blocks = refs[:-4]
    ctx_pos = lax.axis_index("ctx")
    rows = 2 * tok
    if folded:
        listed = each_block(blocks)
        for ref, i, d in listed:
            shard = w.shape[0] // len(listed)
            rest = shard - folded
            lead = (ctx_pos ^ d) * shard
            w[pl.ds(pl.multiple_of(lead, 16), folded), :] = ref[i, rows:, : 3 * hl]
            side = ref[i, rows:, 3 * hl :]
            w[pl.ds(pl.multiple_of(lead + folded, 16), rest), :] = jnp.concatenate(
                [side[t * rest : (t + 1) * rest] for t in range(3)], axis=1
            )
    else:
        w[...] = blocks[-1][...]
        blocks = blocks[:-1]
    listed = each_block(blocks)
    for lead in range(0, len(listed), 4):
        group = listed[lead : lead + 4]
        x = jnp.concatenate([ref[i, :rows, :] for ref, i, _ in group], axis=0).astype(F32)
        normed = (x * rms_scale(x) * gain[...].reshape(1, -1)).astype(BF16)
        full = nn(normed, w[...] if lead == 0 else w[:, hl:]).astype(BF16)
        if lead == 0:
            a_out[...] = normed[:rows]
            q_out[...] = full[:rows, :hl]
            full = full[:, hl:]
        for t, (_, _, d) in enumerate(group):
            kv_out[ctx_pos ^ d] = full[t * rows : (t + 1) * rows].reshape(2, tok, 2 * hl)


def attend_body(heads, q, table, rev, kv_out, o_out, low_out, p_out):
    ctx_pos, exp_pos = lax.axis_index("ctx"), lax.axis_index("exp")
    rows = q.shape[0]
    tok = rows // 2
    hl = heads * HD
    seq_len = rev.shape[1]
    start = ctx_pos * tok
    head_total, buckets = table.shape
    pick = jnp.where(
        iota((8, head_total), 1) == exp_pos * heads + iota((8, head_total), 0), 1.0, 0.0
    )
    own_table = nn(pick, table[...], HIGH)
    hot = jnp.where(iota((buckets, seq_len), 0) == rev[...], 1.0, 0.0)
    bias = pltpu.roll(nn(own_table, hot, HIGH), start + 1, 1)
    open_keys = iota((tok, seq_len), 1) <= start + iota((tok, seq_len), 0)
    skewed = []
    for h in range(heads):
        wide = jnp.broadcast_to(bias[h : h + 1, :], (tok, seq_len))
        turned = pltpu.roll(wide, 0, 1, stride=1, stride_axis=0)
        skewed.append(jnp.where(open_keys, turned, FLOOR))
    halves = []
    for s in range(2):
        outs = []
        for h in range(heads):
            query = q[s * tok : (s + 1) * tok, h * HD : (h + 1) * HD]
            key = kv_out[:, s, :, h * HD : (h + 1) * HD].reshape(seq_len, HD)
            value = kv_out[:, s, :, hl + h * HD : hl + (h + 1) * HD].reshape(seq_len, HD)
            scores = nt(query, key) * (HD**-0.5) + skewed[h]
            top = jnp.max(scores, axis=-1, keepdims=True)
            weights = jnp.exp(scores - top)
            probs = weights * (1.0 / jnp.sum(weights, axis=-1, keepdims=True))
            p_out[s * heads + h] = probs
            outs.append(nn(probs.astype(BF16), value))
        out = jnp.concatenate(outs, axis=1)
        o_out[s * tok : (s + 1) * tok, :] = out
        halves.append(out.astype(BF16))
    packed = fold_lanes(jnp.concatenate(halves, axis=0))
    low_out[...] = packed


def gate_values(logits, info):
    route0, route1 = info[0:1].astype(jnp.int32), info[1:2].astype(jnp.int32)
    choice0 = jnp.zeros_like(info[0:1])
    choice1 = jnp.zeros_like(info[0:1])
    for e in range(logits.shape[0]):
        choice0 = choice0 + jnp.where(route0 == e, logits[e : e + 1], 0.0)
        choice1 = choice1 + jnp.where(route1 == e, logits[e : e + 1], 0.0)
    top = jnp.maximum(choice0, choice1)
    up0, up1 = jnp.exp(choice0 - top), jnp.exp(choice1 - top)
    total = up0 + up1
    return up0 / total, up1 / total


def route_body(tok, quarter, cap, parts, *refs):
    x, mats = refs[:2]
    lows = refs[2 : 2 + parts]
    gain, router_t, info_ref, resid_out, gates_out, slots_out = refs[2 + parts :]
    exp_pos = lax.axis_index("exp")
    rows, width = 2 * tok, gain.shape[0]
    attn = nt(
        jnp.concatenate(
            [unfold_lanes(low[...], rows, mats.shape[1] // parts) for low in lows], axis=1
        ),
        mats[...],
    )
    for s in range(2):
        resid_out[s * tok : (s + 1) * tok, :] = (
            x[s * tok : (s + 1) * tok, :].astype(F32) + attn[s * tok : (s + 1) * tok]
        )
    resid = resid_out[...]
    normed = (resid * rms_scale(resid) * gain[...].reshape(1, -1)).astype(BF16)
    logits = nt(router_t[...], normed.astype(F32), HIGH)
    info = info_ref[...]
    soft0, soft1 = gate_values(logits, info)
    gate0, gate1 = info[2:3] * soft0, info[3:4] * soft1
    gates_out[...] = jnp.concatenate([gate0, gate1, jnp.zeros((6, rows), F32)], axis=0)
    route0, route1 = info[0:1].astype(jnp.int32), info[1:2].astype(jnp.int32)
    before = block_before(rows, tok, quarter)
    hot, _ = slot_hot(route0, route1, exp_pos, before, tok, quarter, cap, parts)
    hot = jnp.where(hot, 1.0, 0.0).astype(BF16)
    first = route0 == exp_pos
    gate = jnp.where(first, gate0, gate1)
    slope = soft0 * soft1 * jnp.where(first, info[2:3], info[3:4])
    other = jnp.where(first, info[1:2], info[0:1])
    gate_hi, slope_hi = gate.astype(BF16).astype(F32), slope.astype(BF16).astype(F32)
    extras = jnp.concatenate(
        [gate_hi, gate - gate_hi, slope_hi, slope - slope_hi, other, jnp.zeros((LANES - 5, rows), F32)],
        axis=0,
    ).astype(BF16)
    slots_out[:, :width] = nn(hot, normed).astype(BF16)
    slots_out[:, width:] = nt(hot, extras).astype(BF16)


def expert_back_body(count, *refs):
    xs, cs = refs[:count], refs[count : 2 * count]
    w_in, down, router_t, near_out, far_out, hid, dg_out, du_out, spread_out = refs[2 * count :]
    exp_pos = lax.axis_index("exp")
    width, hidden = w_in.shape[0], down.shape[0]
    experts = router_t.shape[0]
    gate_w, up_w = w_in[:, :hidden], w_in[:, hidden:]
    down_w = down[...]
    done = 0
    side = near_out.shape[0]
    for x_group, c_group in zip(grouped(xs), grouped(cs)):
        rows = stack(x_group, cols=slice(0, width))
        extras = stack(x_group, cols=slice(width, None)).astype(F32)
        step = rows.shape[0]
        part = slice(done, done + step)
        done = done + step
        gate = extras[:, 0:1] + extras[:, 1:2]
        slope = extras[:, 2:3] + extras[:, 3:4]
        other = extras[:, 4:5].astype(jnp.int32)
        pre = nn(rows, gate_w)
        up = nn(rows, up_w)
        raw = nt(stack(c_group, slice(0, xs[0].shape[1])), down_w)
        squared = pre * pre
        tanh = jnp.tanh(GELU_C * (pre + GELU_A * pre * squared))
        half = 0.5 * (1.0 + tanh)
        act = pre * half
        hidden_low = (act * up).astype(BF16)
        hid[part, :] = hidden_low
        slope_act = half + 0.5 * pre * (1.0 - tanh * tanh) * (
            GELU_C * (1.0 + 3.0 * GELU_A * squared)
        )
        gate_grad = jnp.sum(hidden_low.astype(F32) * raw, axis=-1, keepdims=True)
        grad = gate * raw
        dg = (grad * up * slope_act).astype(BF16)
        du = (grad * act).astype(BF16)
        dg_out[part, :] = dg
        du_out[part, :] = du
        tilt = gate_grad * slope
        kind = iota((step, 8), 1)
        spread = jnp.where(kind == exp_pos, tilt, 0.0) - jnp.where(kind == other, tilt, 0.0)
        spread_out[part, :] = spread
        back = nt(dg, gate_w) + nt(du, up_w)
        for e in range(experts):
            back = back + spread[:, e : e + 1] * router_t[e : e + 1, :]
        out, lead = (near_out, done - step) if done <= side else (far_out, done - step - side)
        out[lead : lead + step, :width] = back.astype(BF16)
        out[lead : lead + step, width:] = nn(hidden_low, down_w).astype(BF16)


def expert_weights_body(count, *refs):
    xs = refs[:count]
    dg, du, *w_outs, wide = refs[count:]
    width = wide.shape[0] * wide.shape[1]
    gate_sum, up_sum = 0.0, 0.0
    done = 0
    for x_group in grouped(xs):
        rows = stack(x_group, cols=slice(0, width))
        part = slice(done, done + rows.shape[0])
        done = done + rows.shape[0]
        gate_sum = gate_sum + tn(rows, dg[part, :])
        up_sum = up_sum + tn(rows, du[part, :])
    w_grad = jnp.concatenate([gate_sum.astype(BF16), up_sum.astype(BF16)], axis=1)
    if len(w_outs) == 1:
        w_outs[0][...] = w_grad.reshape(w_outs[0].shape)
        return
    ctx_pos = lax.axis_index("ctx")
    wide[...] = w_grad.reshape(wide.shape)
    for d, out in enumerate(w_outs):
        out[...] = wide[ctx_pos ^ d]


def expert_rest_body(count, *refs):
    xs, cs = refs[:count], refs[count : 2 * count]
    hid, spread, down_out, router_out = refs[2 * count :]
    width = down_out.shape[1]
    down_sum, router_sum = 0.0, 0.0
    done = 0
    for x_group, c_group in zip(grouped(xs), grouped(cs)):
        rows = stack(x_group, cols=slice(0, width))
        extras = stack(x_group, cols=slice(width, None)).astype(F32)
        part = slice(done, done + rows.shape[0])
        done = done + rows.shape[0]
        gate = extras[:, 0:1] + extras[:, 1:2]
        cot = stack(c_group, slice(0, xs[0].shape[1]))
        dy = (gate * cot.astype(F32)).astype(BF16)
        down_sum = down_sum + tn(hid[part, :], dy)
        router_sum = router_sum + tn(spread[part, :], rows.astype(F32), HIGH)
    down_out[...] = down_sum
    router_out[...] = router_sum


def widen_body(*refs):
    blocks, (gate_out, up_out) = refs[:-2], refs[-2:]
    hidden = blocks[0].shape[-1] // 2
    if len(blocks) == 1:
        for c in range(blocks[0].shape[0]):
            gate_out[:, c * hidden : (c + 1) * hidden] = blocks[0][c, :, :hidden].astype(F32)
            up_out[:, c * hidden : (c + 1) * hidden] = blocks[0][c, :, hidden:].astype(F32)
        return
    ctx_pos = lax.axis_index("ctx")
    for d, block in enumerate(blocks):
        spot = pl.ds(pl.multiple_of((ctx_pos ^ d) * hidden, LANES), hidden)
        gate_out[:, spot] = block[:, :hidden].astype(F32)
        up_out[:, spot] = block[:, hidden:].astype(F32)


def mix_body(tok, quarter, cap, parts, resid, info_ref, gates_ref, ys, out, held, wide):
    exp_pos = lax.axis_index("exp")
    rows, width = 2 * tok, resid.shape[1]
    info, gates = info_ref[...], gates_ref[...]
    route0, route1 = info[0:1].astype(jnp.int32), info[1:2].astype(jnp.int32)
    before = block_before(rows, tok, quarter)
    block = (iota((1, rows), 1) % tok) // quarter
    weights = []
    for e in range(parts):
        named = ((route0 == e) | (route1 == e)) & (block == exp_pos)
        flags = jnp.broadcast_to(jnp.where(named, 1.0, 0.0), (16, rows)).astype(BF16)
        rank = jnp.where(named, nn(flags, before)[0:1].astype(jnp.int32), -1)
        gate = jnp.where(route0 == e, gates[0:1], gates[1:2])
        weights.append(jnp.where(iota((cap, rows), 0) == rank, gate, 0.0))
    weights = jnp.concatenate(weights, axis=0)
    hi = weights.astype(BF16)
    low = (weights - hi.astype(F32)).astype(BF16)
    y = jnp.concatenate(
        [ys[e].astype(F32)[parts * cap :] for e in range(parts)], axis=0
    ).astype(BF16)
    held[...] = resid[...] + tn(hi, y) + tn(low, y)
    for s in range(2):
        spot = pl.ds(pl.multiple_of(s * tok + exp_pos * quarter, quarter), quarter)
        wide[:, s, :] = held[spot, :]
    out[...] = wide[...].astype(BF16)


def attend_back_body(heads, tok, quarter, cap, parts, *refs):
    (
        returned, resid_ref, cot, gain, info_ref, o, out_t, q, kv, p,
        own_out, dq_out, near_out, far_out, grad_out, sums_out, small_out, held, dkv,
    ) = refs
    ctx_pos, exp_pos = lax.axis_index("ctx"), lax.axis_index("exp")
    rows, width = resid_ref.shape
    hl = heads * HD
    count = kv.shape[0]
    seq_len = count * tok
    start = ctx_pos * tok
    info = info_ref[...]
    route0, route1 = info[0:1].astype(jnp.int32), info[1:2].astype(jnp.int32)
    before = block_before(rows, tok, quarter)
    grad = jnp.zeros((rows, width), F32)
    for e in range(parts):
        hot, _ = slot_hot(route0, route1, e, before, tok, quarter, cap, parts)
        piece = returned[e].astype(F32)[: parts * cap].astype(BF16)
        grad = grad + tn(jnp.where(hot, 1.0, 0.0).astype(BF16), piece)
    resid = resid_ref[...]
    scale = rms_scale(resid)
    centred = resid * scale
    small_out[...] = jnp.broadcast_to(
        jnp.sum(grad * centred, axis=0, keepdims=True) * (1.0 / parts), small_out.shape
    )
    inner = grad * gain[...].reshape(1, -1)
    held[...] = cot[...].astype(F32) + scale * (
        inner - centred * jnp.mean(inner * centred, axis=-1, keepdims=True)
    )
    for s in range(2):
        spot = pl.ds(pl.multiple_of(s * tok + exp_pos * quarter, quarter), quarter)
        own_out[s * quarter : (s + 1) * quarter, :] = held[spot, :]
    attn_grad = held[...].astype(BF16)
    grad_o = nn(attn_grad, out_t[...]).astype(BF16)
    grad_out[...] = attn_grad
    sums = [jnp.zeros((tok, seq_len), F32) for _ in range(heads)]
    for s in range(2):
        here = slice(s * tok, (s + 1) * tok)
        keys, values, queries = [], [], []
        for h in range(heads):
            cols = slice(h * HD, (h + 1) * HD)
            probs = p[s * heads + h]
            key = kv[:, s, :, cols].reshape(seq_len, HD)
            value = kv[:, s, :, hl + h * HD : hl + (h + 1) * HD].reshape(seq_len, HD)
            do = grad_o[here, cols]
            delta = jnp.sum(do.astype(F32) * o[here, cols], axis=-1, keepdims=True)
            ds = (probs * (nt(do, value) - delta)).astype(BF16)
            sums[h] = sums[h] + ds.astype(F32)
            values.append(tn(probs.astype(BF16), do).astype(BF16))
            keys.append((tn(ds, q[here, cols]) * (HD**-0.5)).astype(BF16))
            queries.append(nn(ds, key) * (HD**-0.5))
        dq_out[here, :] = jnp.concatenate(queries, axis=1).astype(BF16)
        dkv[:, s] = jnp.concatenate(keys + values, axis=1).reshape(count, tok, 2 * hl)
    for j in range(count // 2):
        near_out[j] = dkv[ctx_pos ^ (2 * j)].reshape(rows, 2 * hl)
        far_out[j] = dkv[ctx_pos ^ (2 * j + 1)].reshape(rows, 2 * hl)
    for h in range(heads):
        sums_out[h] = sums[h]


def table_body(buckets, sums, attn_grad, low, rev, table_out, dout_t):
    ctx_pos, exp_pos = lax.axis_index("ctx"), lax.axis_index("exp")
    heads, tok, seq_len = sums.shape
    width = table_out.shape[1]
    start = ctx_pos * tok
    dout_t[...] = tn(
        attn_grad[...], unfold_lanes(low[...], attn_grad.shape[0], dout_t.shape[1])
    ).astype(BF16)
    lines = []
    for h in range(heads):
        turned = sums[h]
        step = 1
        while step < tok:
            bit = (iota((tok, seq_len), 0) // step) % 2 == 1
            turned = jnp.where(bit, pltpu.roll(turned, seq_len - step, 1), turned)
            step *= 2
        lines.append(jnp.sum(turned, axis=0, keepdims=True))
    lines = jnp.concatenate(lines + [jnp.zeros((8 - heads, seq_len), F32)], axis=0)
    lines = pltpu.roll(lines, seq_len - start - 1, 1)
    counts = jnp.zeros((8, LANES), F32)
    for lead in range(0, seq_len, 512):
        cut = slice(lead, min(lead + 512, seq_len))
        here = lines[:, cut]
        hot = jnp.where(iota((here.shape[1], LANES), 1) == rev[cut, :], 1.0, 0.0)
        counts = counts + nn(here, hot, HIGH)
    table = jnp.zeros((8, width), F32)
    for h in range(heads):
        spot = (exp_pos * heads + h) * buckets
        place = jnp.where(
            (iota((LANES, width), 1) == spot + iota((LANES, width), 0))
            & (iota((LANES, width), 0) < buckets),
            1.0,
            0.0,
        )
        table = table + nn(jnp.broadcast_to(counts[h : h + 1], (8, LANES)), place, HIGH)
    table_out[...] = table


def back_project_body(quarter, parts, *refs):
    da_out, w_near, w_far, small_out, wide = refs[-5:]
    dq, w, a, dout_t, x, gain, small, table, router = refs[:9]
    terms = refs[9:-5]
    ctx_pos, exp_pos = lax.axis_index("ctx"), lax.axis_index("exp")
    rows, width = a.shape
    tok = rows // 2
    dkv = terms[0][...].astype(F32)
    for term in terms[1:]:
        dkv = dkv + term[...].astype(F32)
    grads = jnp.concatenate([dq[...], dkv.astype(BF16)], axis=1)
    da = nt(grads, w[...])
    total = jnp.zeros((1, width), F32)
    for s in range(2):
        piece = x[s * tok : (s + 1) * tok, :].astype(F32)
        here = da[s * tok : (s + 1) * tok]
        total = total + jnp.sum(piece * rms_scale(piece) * here, axis=0, keepdims=True)
        for z in range(parts):
            da_out[z, s * quarter : (s + 1) * quarter, :] = here[
                z * quarter : (z + 1) * quarter
            ].astype(BF16)
    small_out[0:1, :] = total
    small_out[1:2, :] = small[0:1, :]
    small_out[2:3, :] = table[0:1, :]
    small_out[3:7, :] = router[0:4, :]
    small_out[7:8, :] = jnp.zeros((1, width), F32)
    full = jnp.concatenate([tn(a[...], grads).astype(BF16), dout_t[...]], axis=1)
    if len(wide.shape) == 2:
        wide[...] = full
        w_near[...] = full
        w_far[...] = full
        return
    count, shard, _ = wide.shape
    wide[...] = full.reshape(wide.shape)
    for j in range(count // 2):
        w_near[j] = wide[ctx_pos ^ (2 * j)]
        w_far[j] = wide[ctx_pos ^ (2 * j + 1)]


def finish_body(tok, quarter, x, gain, own, pieces, out):
    exp_pos = lax.axis_index("exp")
    width = gain.shape[0]
    for s in range(2):
        spot = pl.ds(pl.multiple_of(s * tok + exp_pos * quarter, quarter), quarter)
        rows = x[spot, :].astype(F32)
        here = slice(s * quarter, (s + 1) * quarter)
        grad = pieces[0, here, :].astype(F32)
        for z in range(1, pieces.shape[0]):
            grad = grad + pieces[z, here, :].astype(F32)
        scale = rms_scale(rows)
        centred = rows * scale
        inner = grad * gain[...].reshape(1, -1)
        out[:, s, :] = own[here, :] + scale * (
            inner - centred * jnp.mean(inner * centred, axis=-1, keepdims=True)
        )


def last_body(count, tok, quarter, x, gain, own, pieces, *refs):
    terms, smalls = refs[:count], refs[count:-9]
    finish_out, q_out, k_out, v_out, o_out, attn_out, ffn_out, table_out, router_out = refs[-9:]
    finish_body(tok, quarter, x, gain, own, pieces, finish_out)
    hl = q_out.shape[1]
    total = terms[0][...].astype(F32)
    for term in terms[1:]:
        total = total + term[...].astype(F32)
    q_out[...] = total[:, :hl]
    k_out[...] = total[:, hl : 2 * hl]
    v_out[...] = total[:, 2 * hl : 3 * hl]
    o_out[...] = total[:, 3 * hl :].T
    small = smalls[0][...]
    for term in smalls[1:]:
        small = small + term[...]
    attn_out[...] = small[0]
    ffn_out[...] = small[1]
    heads, buckets = table_out.shape
    for h in range(heads):
        table_out[h : h + 1, :] = small[2:3, h * buckets : (h + 1) * buckets]
    router_out[...] = small[3 : 3 + router_out.shape[0], :]


def on_device(
    block_input,
    output_cotangent,
    attn_gain,
    query_weight,
    key_weight,
    value_weight,
    output_weight,
    bias_table,
    buckets,
    ffn_gain,
    router_weight,
    routes,
    route_prior,
    gate_weight,
    up_weight,
    down_weight,
):
    tok, seqs, width = block_input.shape
    quarter = routes.shape[0]
    ctx_size, parts = lax.axis_size("ctx"), lax.axis_size("exp")
    hl = query_weight.shape[1]
    heads = hl // HD
    cap = (3 * quarter * seqs + 3) // 4
    slots = parts * cap
    rows = tok * seqs
    shard = query_weight.shape[0]
    hidden = down_weight.shape[1]
    half = ctx_size // 2
    seq_len = tok * ctx_size
    aligned = shard % 16 == 0
    gain_one, gain_two = attn_gain, ffn_gain
    router_t = router_weight.T
    rev = buckets[::-1].reshape(1, seq_len)
    down = down_weight.reshape(hidden, width)

    folded = shard * 5 // 6 if shard % 96 == 0 else 0
    info = jnp.concatenate([routes.astype(F32), route_prior], axis=2).reshape(quarter, 4 * seqs)
    cot_pack, x = call(
        functools.partial(pack_body, folded),
        "pack",
        [
            ((parts, max(3 * seqs * quarter, shard) + 16, width // 3 + hl), BF16),
            ((rows + folded, width), BF16),
        ],
        output_weight, output_cotangent, info, block_input,
        *([query_weight, key_weight, value_weight] if folded else []), us=1.5, wide=True,
    )
    x_blocks = gather_ctx(x)
    if not folded:
        packed = jnp.concatenate([query_weight, key_weight, value_weight], axis=1)
        x_blocks = x_blocks + [lax.all_gather(packed, "ctx", axis=0, tiled=True)]
    cot_packs = trade_exp(cot_pack)
    cot_block, info_block, both_slots = call(
        functools.partial(early_body, tok, quarter, cap),
        "early_slots",
        [
            ((rows, width), BF16),
            ((8, rows), F32),
            ((slots + shard, width), BF16),
        ],
        cot_packs,
    )
    q, kv_all, normed, w_qkv = call(
        functools.partial(project_body, hl, tok, folded),
        "project",
        [
            ((rows, hl), BF16),
            ((ctx_size, seqs, tok, 2 * hl), BF16),
            ((rows, width), BF16),
            ((width, 3 * hl), BF16),
        ],
        gain_one, *x_blocks, us=4.0, after=[info_block], wide=True,
    )
    if aligned:
        c_blocks = gather_ctx(both_slots)
        moved = c_blocks[1:half]
        mats_blocks, mats_lead = c_blocks, slots
    else:
        c_blocks, moved = gather_ctx(both_slots[:slots]), []
        mats_blocks, mats_lead = [lax.all_gather(both_slots[slots:], "ctx", axis=0, tiled=True)], 0

    sent = call(
        functools.partial(sent_body, hidden),
        "sent",
        ((ctx_size, shard, 2 * hidden), BF16),
        gate_weight.reshape(shard, ctx_size * hidden), up_weight.reshape(shard, ctx_size * hidden),
        us=2.0, after=[q],
    )
    mats_full, out_t = call(
        functools.partial(lay_body, mats_lead), "lay_out", [((width, parts * hl), BF16), ((width, hl), BF16)], *mats_blocks,
        us=2.5,
    )
    low_shape = (rows * hl // LANES, LANES) if hl % LANES == LANES // 2 else (rows, hl)
    o, low, p = call(
        functools.partial(attend_body, heads),
        "attend",
        [((rows, hl), F32), (low_shape, BF16), ((seqs * heads, tok, seq_len), F32)],
        q, bias_table.T, rev, kv_all, us=4.8, after=moved, wide=True,
    )
    lows = spread_exp(low)
    w_in = lax.all_to_all(hold(sent, low), "ctx", split_axis=0, concat_axis=0, tiled=True)
    w_in = w_in.reshape(width, 2 * hidden)

    resid, gates, x_slots = call(
        functools.partial(route_body, tok, quarter, cap, parts),
        "route",
        [((rows, width), F32), ((8, rows), F32), ((slots, width + LANES), BF16)],
        x, mats_full, *lows, gain_two, router_t, info_block, us=3.7,
    )
    x_blocks = gather_ctx(x_slots)
    side = half * slots
    cut = len(x_blocks)
    back_near, back_far, hid, dg, du, spread = call(
        functools.partial(expert_back_body, cut),
        "expert_back",
        [((side, 2 * width), BF16)] * 2 + [((2 * side, hidden), BF16)] * 3 + [((2 * side, 8), F32)],
        *x_blocks, *c_blocks, w_in, down, router_t, us=8.0, wide=True,
    )
    back_terms = send_direct(
        add_pair(
            back_near.reshape(half, slots, 2 * width), back_far.reshape(half, slots, 2 * width)
        )
    )
    back_sums, summed = call(
        functools.partial(back_sum_body, cap),
        "sum_back",
        ((parts, slots + cap, width), BF16),
        *back_terms, us=2.0, token=True,
    )
    returned = trade_exp(back_sums)
    by_permutes = ctx_size <= 8 and hidden % LANES == 0
    w_shape = (shard, 2 * hidden)
    *w_grads, weighed = call(
        functools.partial(expert_weights_body, cut),
        "expert_weights",
        [(w_shape, BF16)] * ctx_size if by_permutes else [((ctx_size, *w_shape), BF16)],
        *x_blocks, dg, du, us=4.0, after=[summed], token=True,
        scratch=[pltpu.VMEM((ctx_size, *w_shape), BF16)],
    )
    down_grad, router = call(
        functools.partial(expert_rest_body, cut),
        "expert_rest",
        [((hidden, width), F32), ((8, width), F32)],
        *x_blocks, *c_blocks, hid, spread, us=3.0, after=[weighed],
    )
    if by_permutes:
        w_back = [w_grads[0]] + [swap(w_grads[d], "ctx", d) for d in range(1, ctx_size)]
    else:
        w_back = [lax.all_to_all(w_grads[0], "ctx", split_axis=0, concat_axis=0, tiled=True)]
    gate_grad, up_grad, widened = call(
        widen_body,
        "widen",
        [((shard, ctx_size * hidden), F32)] * 2,
        *w_back, us=2.0, token=True,
    )
    resid_grad, dq, dkv_near, dkv_far, attn_grad, score_sums, small = call(
        functools.partial(attend_back_body, heads, tok, quarter, cap, parts),
        "attend_back",
        [
            ((seqs * quarter, width), F32),
            ((rows, hl), BF16),
            ((half, rows, 2 * hl), BF16),
            ((half, rows, 2 * hl), BF16),
            ((rows, width), BF16),
            ((heads, tok, seq_len), F32),
            ((8, width), F32),
        ],
        returned, resid, cot_block, gain_two, info_block, o, out_t, q, kv_all, p,
        us=8.0,
        scratch=[
            pltpu.VMEM((rows, width), F32),
            pltpu.VMEM((ctx_size, seqs, tok, 2 * hl), BF16),
        ],
        after=[widened, router], wide=True,
    )
    dkv_both = add_pair(dkv_near, dkv_far)
    dkv_terms = send_direct(dkv_both)
    block_output, mixed = call(
        functools.partial(mix_body, tok, quarter, cap, parts),
        "mix",
        ((quarter, seqs, width), BF16),
        resid, info_block, gates, returned,
        scratch=[pltpu.VMEM((rows, width), F32), pltpu.VMEM((quarter, seqs, width), F32)],
        token=True,
        after=[dkv_both[0]],
    )
    table, dout_t = call(
        functools.partial(table_body, bias_table.shape[0]),
        "table",
        [((8, width), F32), ((width, hl), BF16)],
        score_sums, attn_grad, low, rev.reshape(seq_len, 1), us=3.0, after=[dkv_both[0]],
    )
    w_shape = (half, shard, 4 * hl) if aligned else (width, 4 * hl)
    da_parts, w_near, w_far, small = call(
        functools.partial(back_project_body, quarter, parts),
        "back_project",
        [((parts, seqs * quarter, width), BF16)]
        + [(w_shape, BF16), (w_shape, BF16), ((8, width), F32)],
        dq, w_qkv, normed, dout_t, x, gain_one, small, table, router, *dkv_terms, us=3.4,
        scratch=[
            pltpu.VMEM((ctx_size, shard, 4 * hl) if aligned else (width, 4 * hl), BF16),
        ],
        after=[mixed],
    )
    da_terms = trade_exp(da_parts)
    if aligned:
        w_both = add_pair(w_near, w_far)
        w_terms = send_direct(w_both)
    else:
        w_terms = [lax.psum_scatter(w_near.astype(F32), "ctx", scatter_dimension=0, tiled=True)]
    small = sum(spread_exp(small))
    small = small + swap(small, "ctx", 1)
    smalls = [small] + [swap(small, "ctx", 2 * j) for j in range(1, half)]
    buckets_total, head_total = bias_table.shape
    (
        input_grad, query_grad, key_grad, value_grad, output_grad,
        attn_gain_grad, ffn_gain_grad, table_grad, router_grad,
    ) = call(
        functools.partial(last_body, len(w_terms), tok, quarter),
        "last",
        [((quarter, seqs, width), F32)] + [((shard, hl), F32)] * 3
        + [((hl, shard), F32), ((width,), F32), ((width,), F32)]
        + [((head_total, buckets_total), F32), ((router_t.shape[0], width), F32)],
        x, gain_one, resid_grad, da_terms, *w_terms, *smalls, us=2.5,
    )
    return (
        block_output,
        input_grad,
        attn_gain_grad,
        query_grad,
        key_grad,
        value_grad,
        output_grad,
        table_grad.T,
        ffn_gain_grad,
        router_grad.T,
        gate_grad[None],
        up_grad[None],
        down_grad.reshape(1, hidden, width),
    )


def solution(mesh):
    return jax.shard_map(
        on_device,
        mesh=mesh,
        in_specs=(
            P("ctx", None, None),
            P(("ctx", "exp"), None, None),
            P(),
            P("ctx", "exp"),
            P("ctx", "exp"),
            P("ctx", "exp"),
            P("exp", "ctx"),
            P(),
            P(),
            P(),
            P(),
            P(("ctx", "exp"), None, None),
            P(("ctx", "exp"), None, None),
            P("exp", "ctx", None),
            P("exp", "ctx", None),
            P("exp", "ctx", None),
        ),
        out_specs=(
            P(("ctx", "exp"), None, None),
            P(("ctx", "exp"), None, None),
            P(),
            P("ctx", "exp"),
            P("ctx", "exp"),
            P("ctx", "exp"),
            P("exp", "ctx"),
            P(),
            P(),
            P(),
            P("exp", "ctx", None),
            P("exp", "ctx", None),
            P("exp", "ctx", None),
        ),
        check_vma=False,
    )
```

```python
import functools

import jax
import jax.numpy as jnp
from jax import lax
from jax.experimental import pallas as pl
from jax.experimental.pallas import tpu as pltpu
from jax.sharding import PartitionSpec as P

HD = 64
EPS = 1e-06
FLOOR = -1e30
HIGH = lax.Precision.HIGHEST
F32 = jnp.float32
BF16 = jnp.bfloat16
LANES = 128
GELU_C = 0.7978845608028654
GELU_A = 0.044715


def swap(value, axis, bits):
    devices = lax.axis_size(axis)
    return lax.ppermute(value, axis, [(i, i ^ bits) for i in range(devices)])


def hold_with_token(value, *after):
    def body(*refs):
        refs[-1][...] = jnp.zeros(refs[-1].shape, F32)

    return pl.pallas_call(
        body,
        out_shape=[
            jax.ShapeDtypeStruct(value.shape, value.dtype),
            jax.ShapeDtypeStruct((8, LANES), F32),
        ],
        in_specs=[pl.BlockSpec(memory_space=pl.ANY)] * (1 + len(after)),
        out_specs=[pl.BlockSpec(memory_space=pl.ANY), pl.BlockSpec(memory_space=pltpu.VMEM)],
        input_output_aliases={0: 0},
        name="hold",
    )(value, *after)


def gather_ctx(value, after=()):
    devices = lax.axis_size("ctx")
    near = [value[None]] + [swap(value, "ctx", 2 * j)[None] for j in range(1, devices // 2)]
    tokens = []
    if after:
        held = [hold_with_token(block, *after) for block in near[1:]]
        near, tokens = near[:1] + [block for block, _ in held], [token for _, token in held]
    if devices > 8:
        near = [jnp.concatenate(near, axis=0)]
    blocks = near + [swap(block, "ctx", 1) for block in near]
    return (blocks, tokens) if after else blocks


def each_block(refs):
    half = sum(ref.shape[0] for ref in refs) // 2
    listed = [(ref, i) for ref in refs for i in range(ref.shape[0])]
    return [(ref, i, 2 * (t % half) + t // half) for t, (ref, i) in enumerate(listed)]


def grouped(refs):
    listed = [(ref, i) for ref in refs for i in range(ref.shape[0])]
    return [listed[t : t + 4] for t in range(0, len(listed), 4)]


def stack(group, rows=slice(None), cols=slice(None)):
    return jnp.concatenate([ref[i, rows, cols] for ref, i in group], axis=0)


def trade_exp(value):
    return lax.all_to_all(value, "exp", split_axis=0, concat_axis=0, tiled=True)


def spread_exp(value):
    return [value] + [swap(value, "exp", d) for d in range(1, lax.axis_size("exp"))]


def nn(left, right, precision=None):
    return lax.dot_general(
        left, right, (((1,), (0,)), ((), ())), precision=precision, preferred_element_type=F32
    )


def nt(left, right, precision=None):
    return lax.dot_general(
        left, right, (((1,), (1,)), ((), ())), precision=precision, preferred_element_type=F32
    )


def tn(left, right, precision=None):
    return lax.dot_general(
        left, right, (((0,), (0,)), ((), ())), precision=precision, preferred_element_type=F32
    )


def room(shape, dtype):
    *lead, rows, cols = (1, 1, *shape)
    size = jnp.dtype(dtype).itemsize
    tile = 32 // size
    total = -(-rows // tile) * tile * -(-cols // LANES) * LANES * size
    for extent in lead:
        total *= extent
    return total


def call(body, name, outs, *args, us=2.0, scratch=(), after=(), wide=False, token=False):
    single = not isinstance(outs, list)
    outs = ([outs] if single else outs) + ([((8, LANES), F32)] if token else [])
    single = len(outs) == 1
    specs = [pl.BlockSpec(memory_space=pltpu.VMEM)] * len(args)
    specs += [pl.BlockSpec(memory_space=pl.ANY)] * len(after)
    shapes = [jax.ShapeDtypeStruct(*o) for o in outs]
    out_specs = [pl.BlockSpec(memory_space=pltpu.VMEM)] * len(shapes)
    held = sum(room(a.shape, a.dtype) for a in (*args, *shapes))
    held += sum(room(a.shape, a.dtype) for a in scratch)
    limit = min(62 * 2**20, max(16 * 2**20 + 2 * held, 60 * 2**20 if wide else 0))

    def run(*refs):
        rest = refs[len(args) + len(after) :]
        if token:
            place = len(shapes) - 1
            rest[place][...] = jnp.zeros(rest[place].shape, F32)
            rest = rest[:place] + rest[place + 1 :]
        body(*refs[: len(args)], *rest)

    return pl.pallas_call(
        run,
        out_shape=shapes[0] if single else shapes,
        in_specs=specs,
        out_specs=out_specs[0] if single else out_specs,
        scratch_shapes=list(scratch),
        compiler_params=pltpu.CompilerParams(vmem_limit_bytes=limit),
        cost_estimate=pl.CostEstimate(flops=0, bytes_accessed=int(us * 3.0e4), transcendentals=0),
        name=name,
    )(*args, *after)


def hold(value, *after):
    return pl.pallas_call(
        lambda *refs: None,
        out_shape=jax.ShapeDtypeStruct(value.shape, value.dtype),
        in_specs=[pl.BlockSpec(memory_space=pl.ANY)] * (1 + len(after)),
        out_specs=pl.BlockSpec(memory_space=pl.ANY),
        input_output_aliases={0: 0},
        name="hold",
    )(value, *after)


def back_sum_body(cap, *refs):
    terms, out = refs[:-1], refs[-1]
    width = out.shape[2]
    total = terms[0][...].astype(F32)
    for ref in terms[1:]:
        total = total + ref[...].astype(F32)
    for z in range(out.shape[0]):
        y = total[z * cap : (z + 1) * cap, width:]
        out[z] = jnp.concatenate([total[:, :width], y], axis=0).astype(BF16)


def add_pair(near, far):
    got = swap(far, "ctx", 1)
    return [
        (near[j].astype(F32) + got[j].astype(F32)).astype(BF16) for j in range(near.shape[0])
    ]


def send_direct(both):
    return [both[0]] + [swap(block, "ctx", 2 * j) for j, block in enumerate(both) if j > 0]


def rms_scale(values):
    return lax.rsqrt(jnp.mean(values * values, axis=-1, keepdims=True) + EPS)


def iota(shape, axis):
    return lax.broadcasted_iota(jnp.int32, shape, axis)


def block_before(rows, tok, quarter):
    early, late = iota((rows, rows), 0), iota((rows, rows), 1)
    same = (early % tok) // quarter == (late % tok) // quarter
    return jnp.where(same & (early < late), 1.0, 0.0).astype(BF16)


def slot_hot(route0, route1, expert, before, tok, quarter, cap, parts):
    rows = route0.shape[1]
    named = (route0 == expert) | (route1 == expert)
    flags = jnp.broadcast_to(jnp.where(named, 1.0, 0.0), (16, rows)).astype(BF16)
    rank = nn(flags, before)[0:1].astype(jnp.int32)
    block = (iota((1, rows), 1) % tok) // quarter
    place = jnp.where(named, block * cap + rank, -1)
    return iota((parts * cap, rows), 0) == place, named


def pack_body(folded, wo, cot, routes, prior, x, *refs):
    weights, (out, message) = refs[:-2], refs[-2:]
    quarter, shard = cot.shape[0], wo.shape[1]
    width = cot.shape[2]
    tok = x.shape[0]
    wide = x[...].astype(F32)
    for s in range(2):
        message[s * tok : (s + 1) * tok, :] = wide[:, s, :].astype(BF16)
    if folded:
        rest = shard - folded
        cols = 3 * wo.shape[0]
        side = jnp.concatenate([w[folded:, :] for w in weights], axis=0)
        side = jnp.concatenate(
            [side, jnp.zeros((folded - 3 * rest, side.shape[1]), BF16)], axis=0
        )
        message[2 * tok :, :] = jnp.concatenate([w[:folded, :] for w in weights] + [side], axis=1)
    third = width // 3
    rows = 2 * quarter
    out[...] = jnp.zeros(out.shape, BF16)
    first = out.at[0]
    flat = cot[...].astype(F32)
    for s in range(2):
        piece = flat[:, s, :].astype(BF16)
        for c in range(3):
            lead = c * rows + s * quarter
            first[lead : lead + quarter, :third] = piece[:, c * third : (c + 1) * third]
    eye = (iota((shard, shard), 0) == iota((shard, shard), 1)).astype(F32).astype(BF16)
    first[:shard, third:] = nt(eye, wo[...]).astype(BF16)
    choice, weight = routes[...].astype(F32), prior[...]
    total = jnp.zeros((16, LANES), F32)
    for s in range(2):
        values = jnp.concatenate(
            [choice[:, 2 * s : 2 * s + 2], weight[:, 2 * s : 2 * s + 2]], axis=1
        )
        hi = values.astype(BF16).astype(F32)
        mid = (values - hi).astype(BF16).astype(F32)
        terms = [hi, mid, values - hi - mid]
        stacked = jnp.concatenate(terms + [jnp.zeros((quarter, 4), F32)], axis=1).astype(BF16)
        spot = iota((quarter, LANES), 0) + s * quarter == iota((quarter, LANES), 1)
        total = total + tn(stacked, jnp.where(spot, 1.0, 0.0).astype(BF16))
    first[out.shape[1] - 16 :, :LANES] = total.astype(BF16)
    for z in range(1, out.shape[0]):
        out[z] = first[...]


def sent_body(hidden, gate, up, out):
    for c in range(out.shape[0]):
        out[c, :, :hidden] = gate[:, c * hidden : (c + 1) * hidden]
        out[c, :, hidden:] = up[:, c * hidden : (c + 1) * hidden]


def early_body(tok, quarter, cap, *refs):
    pieces, cot_out, info_out, both_out = refs
    exp_pos = lax.axis_index("exp")
    parts = pieces.shape[0]
    rows = 2 * tok
    third = cot_out.shape[1] // 3
    slots = parts * cap
    shard = both_out.shape[0] - slots
    info = jnp.zeros((16, rows), F32)
    for z in range(parts):
        for s in range(2):
            spot = s * tok + z * quarter
            for c in range(3):
                lead = c * 2 * quarter + s * quarter
                cot_out[spot : spot + quarter, c * third : (c + 1) * third] = pieces[
                    z, lead : lead + quarter, :third
                ]
        lane, row = iota((LANES, rows), 0), iota((LANES, rows), 1)
        target = (lane // quarter) * tok + z * quarter + lane % quarter
        spot = jnp.where((target == row) & (lane < 2 * quarter), 1.0, 0.0).astype(BF16)
        info = info + nn(pieces[z, pieces.shape[1] - 16 :, :LANES], spot)
    both_out[slots:, :] = jnp.concatenate(
        [pieces[exp_pos ^ d, :shard, third:] for d in range(parts)], axis=1
    )
    low = info[0:4] + (info[4:8] + info[8:12])
    info_out[...] = jnp.concatenate([low, jnp.zeros((4, rows), F32)], axis=0)
    before = block_before(rows, tok, quarter)
    route0, route1 = low[0:1].astype(jnp.int32), low[1:2].astype(jnp.int32)
    hot, _ = slot_hot(route0, route1, exp_pos, before, tok, quarter, cap, parts)
    both_out[:slots, :] = nn(jnp.where(hot, 1.0, 0.0).astype(BF16), cot_out[...]).astype(BF16)


def lay_rows(refs, out, lead=0):
    if len(refs) == 1:
        out[...] = refs[0][...]
        return
    ctx_pos = lax.axis_index("ctx")
    for ref, i, d in each_block(refs):
        rows = ref.shape[1] - lead
        out[pl.ds(pl.multiple_of((ctx_pos ^ d) * rows, rows), rows), :] = ref[i, lead:, :]


def lay_body(lead, *refs):
    blocks, (mats_out, own_out) = refs[:-2], refs[-2:]
    lay_rows(blocks, mats_out, lead)
    own_out[...] = mats_out[:, : own_out.shape[1]]


def fold_lanes(value):
    rows, cols = value.shape
    if cols % LANES != LANES // 2:
        return value
    whole = [value[:, c : c + LANES] for c in range(0, cols - LANES // 2, LANES)]
    tail = value[:, cols - LANES // 2 :]
    tail = jnp.concatenate([tail[: rows // 2], tail[rows // 2 :]], axis=1)
    return jnp.concatenate(whole + [tail], axis=0)


def unfold_lanes(value, rows, cols):
    if cols % LANES != LANES // 2:
        return value
    count = cols // LANES
    whole = [value[c * rows : (c + 1) * rows] for c in range(count)]
    tail = value[count * rows :]
    tail = jnp.concatenate([tail[:, : LANES // 2], tail[:, LANES // 2 :]], axis=0)
    return jnp.concatenate(whole + [tail], axis=1)


def project_body(hl, tok, folded, gain, *refs):
    q_out, kv_out, a_out, w = refs[-4:]
    blocks = refs[:-4]
    ctx_pos = lax.axis_index("ctx")
    rows = 2 * tok
    if folded:
        listed = each_block(blocks)
        for ref, i, d in listed:
            shard = w.shape[0] // len(listed)
            rest = shard - folded
            lead = (ctx_pos ^ d) * shard
            w[pl.ds(pl.multiple_of(lead, 16), folded), :] = ref[i, rows:, : 3 * hl]
            side = ref[i, rows:, 3 * hl :]
            w[pl.ds(pl.multiple_of(lead + folded, 16), rest), :] = jnp.concatenate(
                [side[t * rest : (t + 1) * rest] for t in range(3)], axis=1
            )
    else:
        w[...] = blocks[-1][...]
        blocks = blocks[:-1]
    listed = each_block(blocks)
    for lead in range(0, len(listed), 4):
        group = listed[lead : lead + 4]
        x = jnp.concatenate([ref[i, :rows, :] for ref, i, _ in group], axis=0).astype(F32)
        normed = (x * rms_scale(x) * gain[...].reshape(1, -1)).astype(BF16)
        full = nn(normed, w[...] if lead == 0 else w[:, hl:]).astype(BF16)
        if lead == 0:
            a_out[...] = normed[:rows]
            q_out[...] = full[:rows, :hl]
            full = full[:, hl:]
        for t, (_, _, d) in enumerate(group):
            kv_out[ctx_pos ^ d] = full[t * rows : (t + 1) * rows].reshape(2, tok, 2 * hl)


def attend_body(heads, q, table, rev, kv_out, o_out, low_out, p_out):
    ctx_pos, exp_pos = lax.axis_index("ctx"), lax.axis_index("exp")
    rows = q.shape[0]
    tok = rows // 2
    hl = heads * HD
    seq_len = rev.shape[1]
    start = ctx_pos * tok
    head_total, buckets = table.shape
    pick = jnp.where(
        iota((8, head_total), 1) == exp_pos * heads + iota((8, head_total), 0), 1.0, 0.0
    )
    own_table = nn(pick, table[...], HIGH)
    hot = jnp.where(iota((buckets, seq_len), 0) == rev[...], 1.0, 0.0)
    bias = pltpu.roll(nn(own_table, hot, HIGH), start + 1, 1)
    open_keys = iota((tok, seq_len), 1) <= start + iota((tok, seq_len), 0)
    skewed = []
    for h in range(heads):
        wide = jnp.broadcast_to(bias[h : h + 1, :], (tok, seq_len))
        turned = pltpu.roll(wide, 0, 1, stride=1, stride_axis=0)
        skewed.append(jnp.where(open_keys, turned, FLOOR))
    halves = []
    for s in range(2):
        outs = []
        for h in range(heads):
            query = q[s * tok : (s + 1) * tok, h * HD : (h + 1) * HD]
            key = kv_out[:, s, :, h * HD : (h + 1) * HD].reshape(seq_len, HD)
            value = kv_out[:, s, :, hl + h * HD : hl + (h + 1) * HD].reshape(seq_len, HD)
            scores = nt(query, key) * (HD**-0.5) + skewed[h]
            top = jnp.max(scores, axis=-1, keepdims=True)
            weights = jnp.exp(scores - top)
            probs = weights * (1.0 / jnp.sum(weights, axis=-1, keepdims=True))
            p_out[s * heads + h] = probs
            outs.append(nn(probs.astype(BF16), value))
        out = jnp.concatenate(outs, axis=1)
        o_out[s * tok : (s + 1) * tok, :] = out
        halves.append(out.astype(BF16))
    packed = fold_lanes(jnp.concatenate(halves, axis=0))
    low_out[...] = packed


def gate_values(logits, info):
    route0, route1 = info[0:1].astype(jnp.int32), info[1:2].astype(jnp.int32)
    choice0 = jnp.zeros_like(info[0:1])
    choice1 = jnp.zeros_like(info[0:1])
    for e in range(logits.shape[0]):
        choice0 = choice0 + jnp.where(route0 == e, logits[e : e + 1], 0.0)
        choice1 = choice1 + jnp.where(route1 == e, logits[e : e + 1], 0.0)
    top = jnp.maximum(choice0, choice1)
    up0, up1 = jnp.exp(choice0 - top), jnp.exp(choice1 - top)
    total = up0 + up1
    return up0 / total, up1 / total


def route_body(tok, quarter, cap, parts, *refs):
    x, mats = refs[:2]
    lows = refs[2 : 2 + parts]
    gain, router_t, info_ref, resid_out, gates_out, slots_out = refs[2 + parts :]
    exp_pos = lax.axis_index("exp")
    rows, width = 2 * tok, gain.shape[0]
    attn = nt(
        jnp.concatenate(
            [unfold_lanes(low[...], rows, mats.shape[1] // parts) for low in lows], axis=1
        ),
        mats[...],
    )
    for s in range(2):
        resid_out[s * tok : (s + 1) * tok, :] = (
            x[s * tok : (s + 1) * tok, :].astype(F32) + attn[s * tok : (s + 1) * tok]
        )
    resid = resid_out[...]
    normed = (resid * rms_scale(resid) * gain[...].reshape(1, -1)).astype(BF16)
    logits = nt(router_t[...], normed.astype(F32), HIGH)
    info = info_ref[...]
    soft0, soft1 = gate_values(logits, info)
    gate0, gate1 = info[2:3] * soft0, info[3:4] * soft1
    gates_out[...] = jnp.concatenate([gate0, gate1, jnp.zeros((6, rows), F32)], axis=0)
    route0, route1 = info[0:1].astype(jnp.int32), info[1:2].astype(jnp.int32)
    before = block_before(rows, tok, quarter)
    hot, _ = slot_hot(route0, route1, exp_pos, before, tok, quarter, cap, parts)
    hot = jnp.where(hot, 1.0, 0.0).astype(BF16)
    first = route0 == exp_pos
    gate = jnp.where(first, gate0, gate1)
    slope = soft0 * soft1 * jnp.where(first, info[2:3], info[3:4])
    other = jnp.where(first, info[1:2], info[0:1])
    gate_hi, slope_hi = gate.astype(BF16).astype(F32), slope.astype(BF16).astype(F32)
    extras = jnp.concatenate(
        [gate_hi, gate - gate_hi, slope_hi, slope - slope_hi, other, jnp.zeros((LANES - 5, rows), F32)],
        axis=0,
    ).astype(BF16)
    slots_out[:, :width] = nn(hot, normed).astype(BF16)
    slots_out[:, width:] = nt(hot, extras).astype(BF16)


def expert_back_body(count, *refs):
    xs, cs = refs[:count], refs[count : 2 * count]
    w_in, down, router_t, near_out, far_out, hid, dg_out, du_out, spread_out = refs[2 * count :]
    exp_pos = lax.axis_index("exp")
    width, hidden = w_in.shape[0], down.shape[0]
    experts = router_t.shape[0]
    gate_w, up_w = w_in[:, :hidden], w_in[:, hidden:]
    down_w = down[...]
    done = 0
    side = near_out.shape[0]
    for x_group, c_group in zip(grouped(xs), grouped(cs)):
        rows = stack(x_group, cols=slice(0, width))
        extras = stack(x_group, cols=slice(width, None)).astype(F32)
        step = rows.shape[0]
        part = slice(done, done + step)
        done = done + step
        gate = extras[:, 0:1] + extras[:, 1:2]
        slope = extras[:, 2:3] + extras[:, 3:4]
        other = extras[:, 4:5].astype(jnp.int32)
        pre = nn(rows, gate_w)
        up = nn(rows, up_w)
        raw = nt(stack(c_group, slice(0, xs[0].shape[1])), down_w)
        squared = pre * pre
        tanh = jnp.tanh(GELU_C * (pre + GELU_A * pre * squared))
        half = 0.5 * (1.0 + tanh)
        act = pre * half
        hidden_low = (act * up).astype(BF16)
        hid[part, :] = hidden_low
        slope_act = half + 0.5 * pre * (1.0 - tanh * tanh) * (
            GELU_C * (1.0 + 3.0 * GELU_A * squared)
        )
        gate_grad = jnp.sum(hidden_low.astype(F32) * raw, axis=-1, keepdims=True)
        grad = gate * raw
        dg = (grad * up * slope_act).astype(BF16)
        du = (grad * act).astype(BF16)
        dg_out[part, :] = dg
        du_out[part, :] = du
        tilt = gate_grad * slope
        kind = iota((step, 8), 1)
        spread = jnp.where(kind == exp_pos, tilt, 0.0) - jnp.where(kind == other, tilt, 0.0)
        spread_out[part, :] = spread
        back = nt(dg, gate_w) + nt(du, up_w)
        for e in range(experts):
            back = back + spread[:, e : e + 1] * router_t[e : e + 1, :]
        out, lead = (near_out, done - step) if done <= side else (far_out, done - step - side)
        out[lead : lead + step, :width] = back.astype(BF16)
        out[lead : lead + step, width:] = nn(hidden_low, down_w).astype(BF16)


def expert_weights_body(count, *refs):
    xs = refs[:count]
    dg, du, *w_outs, wide = refs[count:]
    width = wide.shape[0] * wide.shape[1]
    gate_sum, up_sum = 0.0, 0.0
    done = 0
    for x_group in grouped(xs):
        rows = stack(x_group, cols=slice(0, width))
        part = slice(done, done + rows.shape[0])
        done = done + rows.shape[0]
        gate_sum = gate_sum + tn(rows, dg[part, :])
        up_sum = up_sum + tn(rows, du[part, :])
    w_grad = jnp.concatenate([gate_sum.astype(BF16), up_sum.astype(BF16)], axis=1)
    if len(w_outs) == 1:
        w_outs[0][...] = w_grad.reshape(w_outs[0].shape)
        return
    ctx_pos = lax.axis_index("ctx")
    wide[...] = w_grad.reshape(wide.shape)
    for d, out in enumerate(w_outs):
        out[...] = wide[ctx_pos ^ d]


def expert_rest_body(count, *refs):
    xs, cs = refs[:count], refs[count : 2 * count]
    hid, spread, down_out, router_out = refs[2 * count :]
    width = down_out.shape[1]
    down_sum, router_sum = 0.0, 0.0
    done = 0
    for x_group, c_group in zip(grouped(xs), grouped(cs)):
        rows = stack(x_group, cols=slice(0, width))
        extras = stack(x_group, cols=slice(width, None)).astype(F32)
        part = slice(done, done + rows.shape[0])
        done = done + rows.shape[0]
        gate = extras[:, 0:1] + extras[:, 1:2]
        cot = stack(c_group, slice(0, xs[0].shape[1]))
        dy = (gate * cot.astype(F32)).astype(BF16)
        down_sum = down_sum + tn(hid[part, :], dy)
        router_sum = router_sum + tn(spread[part, :], rows.astype(F32), HIGH)
    down_out[...] = down_sum
    router_out[...] = router_sum


def widen_body(*refs):
    blocks, (gate_out, up_out) = refs[:-2], refs[-2:]
    hidden = blocks[0].shape[-1] // 2
    if len(blocks) == 1:
        for c in range(blocks[0].shape[0]):
            gate_out[:, c * hidden : (c + 1) * hidden] = blocks[0][c, :, :hidden].astype(F32)
            up_out[:, c * hidden : (c + 1) * hidden] = blocks[0][c, :, hidden:].astype(F32)
        return
    ctx_pos = lax.axis_index("ctx")
    for d, block in enumerate(blocks):
        spot = pl.ds(pl.multiple_of((ctx_pos ^ d) * hidden, LANES), hidden)
        gate_out[:, spot] = block[:, :hidden].astype(F32)
        up_out[:, spot] = block[:, hidden:].astype(F32)


def mix_body(tok, quarter, cap, parts, resid, info_ref, gates_ref, ys, out, held, wide):
    exp_pos = lax.axis_index("exp")
    rows, width = 2 * tok, resid.shape[1]
    info, gates = info_ref[...], gates_ref[...]
    route0, route1 = info[0:1].astype(jnp.int32), info[1:2].astype(jnp.int32)
    before = block_before(rows, tok, quarter)
    block = (iota((1, rows), 1) % tok) // quarter
    weights = []
    for e in range(parts):
        named = ((route0 == e) | (route1 == e)) & (block == exp_pos)
        flags = jnp.broadcast_to(jnp.where(named, 1.0, 0.0), (16, rows)).astype(BF16)
        rank = jnp.where(named, nn(flags, before)[0:1].astype(jnp.int32), -1)
        gate = jnp.where(route0 == e, gates[0:1], gates[1:2])
        weights.append(jnp.where(iota((cap, rows), 0) == rank, gate, 0.0))
    weights = jnp.concatenate(weights, axis=0)
    hi = weights.astype(BF16)
    low = (weights - hi.astype(F32)).astype(BF16)
    y = jnp.concatenate(
        [ys[e].astype(F32)[parts * cap :] for e in range(parts)], axis=0
    ).astype(BF16)
    held[...] = resid[...] + tn(hi, y) + tn(low, y)
    for s in range(2):
        spot = pl.ds(pl.multiple_of(s * tok + exp_pos * quarter, quarter), quarter)
        wide[:, s, :] = held[spot, :]
    out[...] = wide[...].astype(BF16)


def attend_back_body(heads, tok, quarter, cap, parts, *refs):
    (
        returned, resid_ref, cot, gain, info_ref, o, out_t, q, kv, p,
        own_out, dq_out, near_out, far_out, grad_out, sums_out, small_out, held, dkv,
    ) = refs
    ctx_pos, exp_pos = lax.axis_index("ctx"), lax.axis_index("exp")
    rows, width = resid_ref.shape
    hl = heads * HD
    count = kv.shape[0]
    seq_len = count * tok
    start = ctx_pos * tok
    info = info_ref[...]
    route0, route1 = info[0:1].astype(jnp.int32), info[1:2].astype(jnp.int32)
    before = block_before(rows, tok, quarter)
    grad = jnp.zeros((rows, width), F32)
    for e in range(parts):
        hot, _ = slot_hot(route0, route1, e, before, tok, quarter, cap, parts)
        piece = returned[e].astype(F32)[: parts * cap].astype(BF16)
        grad = grad + tn(jnp.where(hot, 1.0, 0.0).astype(BF16), piece)
    resid = resid_ref[...]
    scale = rms_scale(resid)
    centred = resid * scale
    small_out[...] = jnp.broadcast_to(
        jnp.sum(grad * centred, axis=0, keepdims=True) * (1.0 / parts), small_out.shape
    )
    inner = grad * gain[...].reshape(1, -1)
    held[...] = cot[...].astype(F32) + scale * (
        inner - centred * jnp.mean(inner * centred, axis=-1, keepdims=True)
    )
    for s in range(2):
        spot = pl.ds(pl.multiple_of(s * tok + exp_pos * quarter, quarter), quarter)
        own_out[s * quarter : (s + 1) * quarter, :] = held[spot, :]
    attn_grad = held[...].astype(BF16)
    grad_o = nn(attn_grad, out_t[...]).astype(BF16)
    grad_out[...] = attn_grad
    sums = [jnp.zeros((tok, seq_len), F32) for _ in range(heads)]
    for s in range(2):
        here = slice(s * tok, (s + 1) * tok)
        keys, values, queries = [], [], []
        for h in range(heads):
            cols = slice(h * HD, (h + 1) * HD)
            probs = p[s * heads + h]
            key = kv[:, s, :, cols].reshape(seq_len, HD)
            value = kv[:, s, :, hl + h * HD : hl + (h + 1) * HD].reshape(seq_len, HD)
            do = grad_o[here, cols]
            delta = jnp.sum(do.astype(F32) * o[here, cols], axis=-1, keepdims=True)
            ds = (probs * (nt(do, value) - delta)).astype(BF16)
            sums[h] = sums[h] + ds.astype(F32)
            values.append(tn(probs.astype(BF16), do).astype(BF16))
            keys.append((tn(ds, q[here, cols]) * (HD**-0.5)).astype(BF16))
            queries.append(nn(ds, key) * (HD**-0.5))
        dq_out[here, :] = jnp.concatenate(queries, axis=1).astype(BF16)
        dkv[:, s] = jnp.concatenate(keys + values, axis=1).reshape(count, tok, 2 * hl)
    for j in range(count // 2):
        near_out[j] = dkv[ctx_pos ^ (2 * j)].reshape(rows, 2 * hl)
        far_out[j] = dkv[ctx_pos ^ (2 * j + 1)].reshape(rows, 2 * hl)
    for h in range(heads):
        sums_out[h] = sums[h]


def table_body(buckets, sums, attn_grad, low, rev, table_out, dout_t):
    ctx_pos, exp_pos = lax.axis_index("ctx"), lax.axis_index("exp")
    heads, tok, seq_len = sums.shape
    width = table_out.shape[1]
    start = ctx_pos * tok
    dout_t[...] = tn(
        attn_grad[...], unfold_lanes(low[...], attn_grad.shape[0], dout_t.shape[1])
    ).astype(BF16)
    lines = []
    for h in range(heads):
        turned = sums[h]
        step = 1
        while step < tok:
            bit = (iota((tok, seq_len), 0) // step) % 2 == 1
            turned = jnp.where(bit, pltpu.roll(turned, seq_len - step, 1), turned)
            step *= 2
        lines.append(jnp.sum(turned, axis=0, keepdims=True))
    lines = jnp.concatenate(lines + [jnp.zeros((8 - heads, seq_len), F32)], axis=0)
    lines = pltpu.roll(lines, seq_len - start - 1, 1)
    counts = jnp.zeros((8, LANES), F32)
    for lead in range(0, seq_len, 512):
        cut = slice(lead, min(lead + 512, seq_len))
        here = lines[:, cut]
        hot = jnp.where(iota((here.shape[1], LANES), 1) == rev[cut, :], 1.0, 0.0)
        counts = counts + nn(here, hot, HIGH)
    table = jnp.zeros((8, width), F32)
    for h in range(heads):
        spot = (exp_pos * heads + h) * buckets
        place = jnp.where(
            (iota((LANES, width), 1) == spot + iota((LANES, width), 0))
            & (iota((LANES, width), 0) < buckets),
            1.0,
            0.0,
        )
        table = table + nn(jnp.broadcast_to(counts[h : h + 1], (8, LANES)), place, HIGH)
    table_out[...] = table


def back_project_body(quarter, parts, *refs):
    da_out, w_near, w_far, small_out, wide = refs[-5:]
    dq, w, a, dout_t, x, gain, small, table, router = refs[:9]
    terms = refs[9:-5]
    ctx_pos, exp_pos = lax.axis_index("ctx"), lax.axis_index("exp")
    rows, width = a.shape
    tok = rows // 2
    dkv = terms[0][...].astype(F32)
    for term in terms[1:]:
        dkv = dkv + term[...].astype(F32)
    grads = jnp.concatenate([dq[...], dkv.astype(BF16)], axis=1)
    da = nt(grads, w[...])
    total = jnp.zeros((1, width), F32)
    for s in range(2):
        piece = x[s * tok : (s + 1) * tok, :].astype(F32)
        here = da[s * tok : (s + 1) * tok]
        total = total + jnp.sum(piece * rms_scale(piece) * here, axis=0, keepdims=True)
        for z in range(parts):
            da_out[z, s * quarter : (s + 1) * quarter, :] = here[
                z * quarter : (z + 1) * quarter
            ].astype(BF16)
    small_out[0:1, :] = total
    small_out[1:2, :] = small[0:1, :]
    small_out[2:3, :] = table[0:1, :]
    small_out[3:7, :] = router[0:4, :]
    small_out[7:8, :] = jnp.zeros((1, width), F32)
    full = jnp.concatenate([tn(a[...], grads).astype(BF16), dout_t[...]], axis=1)
    if len(wide.shape) == 2:
        wide[...] = full
        w_near[...] = full
        w_far[...] = full
        return
    count, shard, _ = wide.shape
    wide[...] = full.reshape(wide.shape)
    for j in range(count // 2):
        w_near[j] = wide[ctx_pos ^ (2 * j)]
        w_far[j] = wide[ctx_pos ^ (2 * j + 1)]


def finish_body(tok, quarter, x, gain, own, pieces, out):
    exp_pos = lax.axis_index("exp")
    width = gain.shape[0]
    for s in range(2):
        spot = pl.ds(pl.multiple_of(s * tok + exp_pos * quarter, quarter), quarter)
        rows = x[spot, :].astype(F32)
        here = slice(s * quarter, (s + 1) * quarter)
        grad = pieces[0, here, :].astype(F32)
        for z in range(1, pieces.shape[0]):
            grad = grad + pieces[z, here, :].astype(F32)
        scale = rms_scale(rows)
        centred = rows * scale
        inner = grad * gain[...].reshape(1, -1)
        out[:, s, :] = own[here, :] + scale * (
            inner - centred * jnp.mean(inner * centred, axis=-1, keepdims=True)
        )


def last_body(count, tok, quarter, x, gain, own, pieces, *refs):
    terms, smalls = refs[:count], refs[count:-9]
    finish_out, q_out, k_out, v_out, o_out, attn_out, ffn_out, table_out, router_out = refs[-9:]
    finish_body(tok, quarter, x, gain, own, pieces, finish_out)
    hl = q_out.shape[1]
    total = terms[0][...].astype(F32)
    for term in terms[1:]:
        total = total + term[...].astype(F32)
    q_out[...] = total[:, :hl]
    k_out[...] = total[:, hl : 2 * hl]
    v_out[...] = total[:, 2 * hl : 3 * hl]
    o_out[...] = total[:, 3 * hl :].T
    small = smalls[0][...]
    for term in smalls[1:]:
        small = small + term[...]
    attn_out[...] = small[0]
    ffn_out[...] = small[1]
    heads, buckets = table_out.shape
    for h in range(heads):
        table_out[h : h + 1, :] = small[2:3, h * buckets : (h + 1) * buckets]
    router_out[...] = small[3 : 3 + router_out.shape[0], :]


def on_device(
    block_input,
    output_cotangent,
    attn_gain,
    query_weight,
    key_weight,
    value_weight,
    output_weight,
    bias_table,
    buckets,
    ffn_gain,
    router_weight,
    routes,
    route_prior,
    gate_weight,
    up_weight,
    down_weight,
):
    tok, seqs, width = block_input.shape
    quarter = routes.shape[0]
    ctx_size, parts = lax.axis_size("ctx"), lax.axis_size("exp")
    hl = query_weight.shape[1]
    heads = hl // HD
    cap = (3 * quarter * seqs + 3) // 4
    slots = parts * cap
    rows = tok * seqs
    shard = query_weight.shape[0]
    hidden = down_weight.shape[1]
    half = ctx_size // 2
    seq_len = tok * ctx_size
    aligned = shard % 16 == 0
    gain_one, gain_two = attn_gain, ffn_gain
    router_t = router_weight.T
    rev = buckets[::-1].reshape(1, seq_len)
    down = down_weight.reshape(hidden, width)

    folded = shard * 5 // 6 if shard % 96 == 0 else 0
    cot_pack, x = call(
        functools.partial(pack_body, folded),
        "pack",
        [
            ((parts, max(3 * seqs * quarter, shard) + 16, width // 3 + hl), BF16),
            ((rows + folded, width), BF16),
        ],
        output_weight, output_cotangent, routes.reshape(quarter, 2 * seqs),
        route_prior.reshape(quarter, 2 * seqs), block_input,
        *([query_weight, key_weight, value_weight] if folded else []), us=1.5, wide=True,
    )
    x_blocks = gather_ctx(x)
    if not folded:
        packed = jnp.concatenate([query_weight, key_weight, value_weight], axis=1)
        x_blocks = x_blocks + [lax.all_gather(packed, "ctx", axis=0, tiled=True)]
    cot_packs = trade_exp(cot_pack)
    cot_block, info_block, both_slots = call(
        functools.partial(early_body, tok, quarter, cap),
        "early_slots",
        [
            ((rows, width), BF16),
            ((8, rows), F32),
            ((slots + shard, width), BF16),
        ],
        cot_packs,
    )
    q, kv_all, normed, w_qkv = call(
        functools.partial(project_body, hl, tok, folded),
        "project",
        [
            ((rows, hl), BF16),
            ((ctx_size, seqs, tok, 2 * hl), BF16),
            ((rows, width), BF16),
            ((width, 3 * hl), BF16),
        ],
        gain_one, *x_blocks, us=4.0, after=[info_block], wide=True,
    )
    if aligned:
        c_blocks = gather_ctx(both_slots)
        moved = c_blocks[1:half]
        mats_blocks, mats_lead = c_blocks, slots
    else:
        c_blocks, moved = gather_ctx(both_slots[:slots]), []
        mats_blocks, mats_lead = [lax.all_gather(both_slots[slots:], "ctx", axis=0, tiled=True)], 0

    sent = call(
        functools.partial(sent_body, hidden),
        "sent",
        ((ctx_size, shard, 2 * hidden), BF16),
        gate_weight.reshape(shard, ctx_size * hidden), up_weight.reshape(shard, ctx_size * hidden),
        us=2.0, after=[q],
    )
    mats_full, out_t = call(
        functools.partial(lay_body, mats_lead), "lay_out", [((width, parts * hl), BF16), ((width, hl), BF16)], *mats_blocks,
        us=2.5,
    )
    low_shape = (rows * hl // LANES, LANES) if hl % LANES == LANES // 2 else (rows, hl)
    o, low, p = call(
        functools.partial(attend_body, heads),
        "attend",
        [((rows, hl), F32), (low_shape, BF16), ((seqs * heads, tok, seq_len), F32)],
        q, bias_table.T, rev, kv_all, us=4.8, after=moved, wide=True,
    )
    lows = spread_exp(low)
    w_in = lax.all_to_all(hold(sent, low), "ctx", split_axis=0, concat_axis=0, tiled=True)
    w_in = w_in.reshape(width, 2 * hidden)

    resid, gates, x_slots = call(
        functools.partial(route_body, tok, quarter, cap, parts),
        "route",
        [((rows, width), F32), ((8, rows), F32), ((slots, width + LANES), BF16)],
        x, mats_full, *lows, gain_two, router_t, info_block, us=3.7,
    )
    x_blocks = gather_ctx(x_slots)
    side = half * slots
    cut = len(x_blocks)
    back_near, back_far, hid, dg, du, spread = call(
        functools.partial(expert_back_body, cut),
        "expert_back",
        [((side, 2 * width), BF16)] * 2 + [((2 * side, hidden), BF16)] * 3 + [((2 * side, 8), F32)],
        *x_blocks, *c_blocks, w_in, down, router_t, us=8.0, wide=True,
    )
    back_terms = send_direct(
        add_pair(
            back_near.reshape(half, slots, 2 * width), back_far.reshape(half, slots, 2 * width)
        )
    )
    by_permutes = ctx_size <= 8 and hidden % LANES == 0
    w_shape = (shard, 2 * hidden)
    *w_grads, weighed = call(
        functools.partial(expert_weights_body, cut),
        "expert_weights",
        [(w_shape, BF16)] * ctx_size if by_permutes else [((ctx_size, *w_shape), BF16)],
        *x_blocks, dg, du, us=4.0, after=[back_terms[0]], token=True,
        scratch=[pltpu.VMEM((ctx_size, *w_shape), BF16)],
    )
    down_grad, router = call(
        functools.partial(expert_rest_body, cut),
        "expert_rest",
        [((hidden, width), F32), ((8, width), F32)],
        *x_blocks, *c_blocks, hid, spread, us=3.0, after=[weighed],
    )
    back_sums, summed = call(
        functools.partial(back_sum_body, cap),
        "sum_back",
        ((parts, slots + cap, width), BF16),
        *back_terms, us=2.0, token=True, after=[router],
    )
    returned = trade_exp(back_sums)
    if by_permutes:
        w_back = [w_grads[0]] + [swap(w_grads[d], "ctx", d) for d in range(1, ctx_size)]
    else:
        w_back = [lax.all_to_all(w_grads[0], "ctx", split_axis=0, concat_axis=0, tiled=True)]
    gate_grad, up_grad, widened = call(
        widen_body,
        "widen",
        [((shard, ctx_size * hidden), F32)] * 2,
        *w_back, us=2.0, token=True,
    )
    resid_grad, dq, dkv_near, dkv_far, attn_grad, score_sums, small = call(
        functools.partial(attend_back_body, heads, tok, quarter, cap, parts),
        "attend_back",
        [
            ((seqs * quarter, width), F32),
            ((rows, hl), BF16),
            ((half, rows, 2 * hl), BF16),
            ((half, rows, 2 * hl), BF16),
            ((rows, width), BF16),
            ((heads, tok, seq_len), F32),
            ((8, width), F32),
        ],
        returned, resid, cot_block, gain_two, info_block, o, out_t, q, kv_all, p,
        us=8.0,
        scratch=[
            pltpu.VMEM((rows, width), F32),
            pltpu.VMEM((ctx_size, seqs, tok, 2 * hl), BF16),
        ],
        after=[widened], wide=True,
    )
    dkv_both = add_pair(dkv_near, dkv_far)
    dkv_terms = send_direct(dkv_both)
    block_output, mixed = call(
        functools.partial(mix_body, tok, quarter, cap, parts),
        "mix",
        ((quarter, seqs, width), BF16),
        resid, info_block, gates, returned,
        scratch=[pltpu.VMEM((rows, width), F32), pltpu.VMEM((quarter, seqs, width), F32)],
        token=True,
        after=[dkv_both[0]],
    )
    table, dout_t = call(
        functools.partial(table_body, bias_table.shape[0]),
        "table",
        [((8, width), F32), ((width, hl), BF16)],
        score_sums, attn_grad, low, rev.reshape(seq_len, 1), us=3.0, after=[dkv_both[0]],
    )
    w_shape = (half, shard, 4 * hl) if aligned else (width, 4 * hl)
    da_parts, w_near, w_far, small = call(
        functools.partial(back_project_body, quarter, parts),
        "back_project",
        [((parts, seqs * quarter, width), BF16)]
        + [(w_shape, BF16), (w_shape, BF16), ((8, width), F32)],
        dq, w_qkv, normed, dout_t, x, gain_one, small, table, router, *dkv_terms, us=3.4,
        scratch=[
            pltpu.VMEM((ctx_size, shard, 4 * hl) if aligned else (width, 4 * hl), BF16),
        ],
        after=[mixed],
    )
    da_terms = trade_exp(da_parts)
    if aligned:
        w_both = add_pair(w_near, w_far)
        w_terms = send_direct(w_both)
    else:
        w_terms = [lax.psum_scatter(w_near.astype(F32), "ctx", scatter_dimension=0, tiled=True)]
    small = sum(spread_exp(small))
    small = small + swap(small, "ctx", 1)
    smalls = [small] + [swap(small, "ctx", 2 * j) for j in range(1, half)]
    buckets_total, head_total = bias_table.shape
    (
        input_grad, query_grad, key_grad, value_grad, output_grad,
        attn_gain_grad, ffn_gain_grad, table_grad, router_grad,
    ) = call(
        functools.partial(last_body, len(w_terms), tok, quarter),
        "last",
        [((quarter, seqs, width), F32)] + [((shard, hl), F32)] * 3
        + [((hl, shard), F32), ((width,), F32), ((width,), F32)]
        + [((head_total, buckets_total), F32), ((router_t.shape[0], width), F32)],
        x, gain_one, resid_grad, da_terms, *w_terms, *smalls, us=2.5,
    )
    return (
        block_output,
        input_grad,
        attn_gain_grad,
        query_grad,
        key_grad,
        value_grad,
        output_grad,
        table_grad.T,
        ffn_gain_grad,
        router_grad.T,
        gate_grad[None],
        up_grad[None],
        down_grad.reshape(1, hidden, width),
    )


def solution(mesh):
    return jax.shard_map(
        on_device,
        mesh=mesh,
        in_specs=(
            P("ctx", None, None),
            P(("ctx", "exp"), None, None),
            P(),
            P("ctx", "exp"),
            P("ctx", "exp"),
            P("ctx", "exp"),
            P("exp", "ctx"),
            P(),
            P(),
            P(),
            P(),
            P(("ctx", "exp"), None, None),
            P(("ctx", "exp"), None, None),
            P("exp", "ctx", None),
            P("exp", "ctx", None),
            P("exp", "ctx", None),
        ),
        out_specs=(
            P(("ctx", "exp"), None, None),
            P(("ctx", "exp"), None, None),
            P(),
            P("ctx", "exp"),
            P("ctx", "exp"),
            P("ctx", "exp"),
            P("exp", "ctx"),
            P(),
            P(),
            P(),
            P("exp", "ctx", None),
            P("exp", "ctx", None),
            P("exp", "ctx", None),
        ),
        check_vma=False,
    )
```
